128 devices in a mesh: dp: 8 (over z, core), ctx: 16 (over x, y).
Axes of the slice: x: 4, y: 4, z: 4, core: 2. Of those that a mesh axis runs over, the one named last changes fastest.
Arguments:
- queries: bfloat16 [8, 2048, 64, 576], P('dp', 'ctx'), may hold values from -29.108076 to 29.108076
- latents: bfloat16 [8, 2048, 576], P('dp', 'ctx'), may hold values from -4.5 to 4.5
- out_grad: bfloat16 [8, 2048, 64, 512], P('dp', 'ctx'), may hold values from -6 to 6
- layer_input: bfloat16 [8, 2048, 5120], P('dp', 'ctx'), may hold values from -0.125 to 0.125
- block_list: int32 [8, 16, 4], P('dp'), may hold values from -1 to 15, as said below
Outputs:
- latent_grad: float32 [8, 2048, 576], P('dp', 'ctx')
- weight_grad: float32 [5120, 576], P('ctx')
The draws below stay inside these ranges and needn't reach their ends.
Inputs may be any that keep to these rules, and one draw needn't show every extreme that they name: `block_list`: row (s, b) lists block b, then the 1 block before it (-1 where they would fall before block 0), then up to 2 distinct blocks drawn among those before the window (-1 in the slots left empty). No row names a block twice.
All inputs are finite; a program needn't handle non-finite values.
Results may differ from the reference program's by a relative error of at most 0.035.
Values may be sent and summed in bfloat16 or wider, within the bound.
A program may use at most 128 MiB of HBM per device.

```python
import jax
import jax.numpy as jnp
from jax import lax

D = 5120
H = 64
R = 512
ROPE = 64
NOPE = 128
TOK_DEV = 128
WINDOW = 2
GLOBALS = 2
SLOTS = 4
KV_WIDTH = 576
SEQ_LEN = 2048
SEQS = 8
N_CTX = 16


def draw_latents(key, part):
    key = jax.random.fold_in(key, 11)
    shape = (SEQS, SEQ_LEN, KV_WIDTH)
    values = jnp.clip(jax.random.normal(key, shape, jnp.float32), -4.5, 4.5)
    return values.astype(jnp.bfloat16)


def draw_queries(key, part):
    key = jax.random.fold_in(key, 12)
    base_key = jax.random.fold_in(key, 0)
    shape = (SEQS, SEQ_LEN, H, KV_WIDTH)
    values = jnp.clip(0.6 * jax.random.normal(base_key, shape, jnp.float32), -3.6, 3.6)
    return values.astype(jnp.bfloat16)


def draw_block_list(key, part):
    key = jax.random.fold_in(key, 13)
    query_block = jnp.arange(N_CTX, dtype=jnp.int32)[:, None]
    window = query_block - jnp.arange(WINDOW, dtype=jnp.int32)[None, :]
    window = jnp.where(window >= 0, window, -1)
    candidate = jnp.arange(N_CTX, dtype=jnp.int32)[None, :]
    allowed = candidate <= query_block - WINDOW
    noise = jax.random.randint(key, (SEQS, N_CTX, N_CTX), 0, 2 ** 20)
    ranking = jnp.where(allowed[None], noise * N_CTX + candidate[None], 2 ** 30 + candidate[None])
    picked = jnp.argsort(ranking, axis=-1)[..., :GLOBALS].astype(jnp.int32)
    available = jnp.maximum(query_block - WINDOW + 1, 0)
    slot = jnp.arange(GLOBALS, dtype=jnp.int32)[None, :]
    chosen = jnp.where((slot < available)[None], picked, -1)
    window_all = jnp.broadcast_to(window[None], (SEQS, N_CTX, WINDOW))
    return jnp.concatenate([window_all, chosen], axis=-1).astype(jnp.int32)


def raised(values, rng, source, target, blocks, factor):
    owner, partner = [(jnp.arange(values.shape[dim]) // (values.shape[dim] // blocks)).reshape([-1 if axis == dim else 1 for axis in range(values.ndim)]) for dim in (source, target)]
    chosen = jax.random.permutation(rng, blocks)[partner]
    strong = (owner == chosen) | (owner == (partner + blocks // 2) % blocks)
    return jnp.where(strong, factor * values, values)


def shard_levels(rng, extent, pieces, smallest, high):
    factor_of = 1.0
    for axis_at, shards_of in pieces:
        draws = jax.random.uniform(jax.random.fold_in(jax.random.fold_in(rng, 6), axis_at), (shards_of,), jnp.float32, smallest / len(pieces), high / len(pieces))
        factor_of = factor_of * jnp.repeat(jnp.exp(draws), extent[axis_at] // shards_of).reshape((-1,) + (1,) * (len(extent) - 1 - axis_at))
    return factor_of


def centred(stream_key, extent, scale, bound, cuts=(), held_as=jnp.bfloat16):
    result = jax.random.normal(stream_key, extent, jnp.float32) * scale
    if len(cuts) > 0:
        result = shard_levels(stream_key, extent, cuts, -0.22, 0.18) * result
    return jnp.clip(result, min=-bound, max=bound).astype(held_as)


def noise_with(key, shape, scale, reach, shards, heavy, held_as=jnp.bfloat16):
    values = scale * jax.random.normal(key, shape, jnp.float32)
    if shards:
        values = values * shard_levels(key, shape, shards, -0.22, 0.18)
    return jnp.clip(raised(values, jax.random.fold_in(key, 3), *heavy), -reach, reach).astype(held_as)


def setup_inputs(seed: int = 0) -> dict:
    keys = jax.random.split(jax.random.key(seed), 6)
    queries = draw_queries(jax.random.fold_in(keys[5], 71), 0)
    latents = draw_latents(jax.random.fold_in(keys[5], 71), 0)
    out_grad = centred(keys[2], (SEQS, SEQ_LEN, H, R), 1.0, 6.0, ((0, 8), (1, 16)))
    layer_input = noise_with(keys[3], (SEQS, SEQ_LEN, D), (2.0 * (SEQS * SEQ_LEN) ** -0.5), 0.125, ((0, 8), (1, 16)), (1, 2, 16, 2.0))
    block_list = draw_block_list(jax.random.fold_in(keys[5], 71), 0)
    return {"queries": queries, "latents": latents, "out_grad": out_grad, "layer_input": layer_input, "block_list": block_list}


def make_visible(row_list, query_block, heads_row, block_len):
    token_row = jnp.arange(block_len * heads_row, dtype=jnp.int32) // heads_row
    position = jnp.arange(SLOTS * block_len, dtype=jnp.int32)
    entry = row_list[position // block_len]
    inner = position % block_len
    listed = (entry >= 0)[None, :]
    earlier = (entry != query_block)[None, :] | (inner[None, :] <= token_row[:, None])
    return listed & earlier


def block_grads(query_rows, grad_rows, keys_flat, visible, scale):
    scores = jnp.dot(query_rows, keys_flat.T, preferred_element_type=jnp.float32) * scale
    scores = jnp.where(visible, scores, -jnp.inf)
    top = jnp.max(scores, axis=1, keepdims=True)
    weights = jnp.exp(scores - top)
    probs = weights / jnp.sum(weights, axis=1, keepdims=True)
    probs_b = probs.astype(jnp.bfloat16)
    values = keys_flat[:, :R]
    output = jnp.dot(probs_b, values, preferred_element_type=jnp.float32)
    delta = jnp.sum(grad_rows.astype(jnp.float32) * output, axis=1, keepdims=True)
    dprob = jnp.dot(grad_rows, values.T, preferred_element_type=jnp.float32)
    dscore = (probs * (dprob - delta) * scale).astype(jnp.bfloat16)
    key_grad = jnp.dot(dscore.T, query_rows, preferred_element_type=jnp.float32)
    value_grad = jnp.dot(probs_b.T, grad_rows, preferred_element_type=jnp.float32)
    return jnp.concatenate([key_grad[:, :R] + value_grad, key_grad[:, R:]], axis=1)


def reference(queries, latents, out_grad, layer_input, block_list):
    scale = (NOPE + ROPE) ** -0.5

    def one_sequence(items):
        seq_queries, seq_latents, seq_grad, seq_list = items
        blocks = seq_latents.reshape(N_CTX, TOK_DEV, KV_WIDTH)

        def one_block(total, query_block):
            start = query_block * TOK_DEV
            query_rows = lax.dynamic_slice_in_dim(seq_queries, start, TOK_DEV, 0).reshape(TOK_DEV * H, KV_WIDTH)
            grad_rows = lax.dynamic_slice_in_dim(seq_grad, start, TOK_DEV, 0).reshape(TOK_DEV * H, R)
            row_list = seq_list[query_block]
            keys_flat = blocks[jnp.maximum(row_list, 0)].reshape(SLOTS * TOK_DEV, KV_WIDTH)
            visible = make_visible(row_list, query_block, H, TOK_DEV)
            parts = block_grads(query_rows, grad_rows, keys_flat, visible, scale)
            one_hot = (jnp.arange(N_CTX, dtype=jnp.int32)[:, None] == row_list[None, :]).astype(jnp.float32)
            spread = jnp.einsum("be,etk->btk", one_hot, parts.reshape(SLOTS, TOK_DEV, KV_WIDTH), precision=lax.Precision.HIGHEST)
            return total + spread, None

        start_total = jnp.zeros((N_CTX, TOK_DEV, KV_WIDTH), jnp.float32)
        total, _ = lax.scan(one_block, start_total, jnp.arange(N_CTX, dtype=jnp.int32))
        return total.reshape(SEQ_LEN, KV_WIDTH)

    latent_grad = lax.map(one_sequence, (queries, latents, out_grad, block_list))
    grad_b = latent_grad.astype(jnp.bfloat16).reshape(SEQS * SEQ_LEN, KV_WIDTH)
    inputs_flat = layer_input.reshape(SEQS * SEQ_LEN, D)
    weight_grad = lax.dot_general(inputs_flat, grad_b, (((0,), (0,)), ((), ())), preferred_element_type=jnp.float32)
    return latent_grad, weight_grad
```

```python
import functools

import jax
import jax.numpy as jnp
from jax import lax
from jax.experimental import pallas as pl
from jax.experimental.pallas import tpu as pltpu
from jax.sharding import PartitionSpec as P

R = 512
W = 576
HALF = 288
TOK = 128
SLOTS = 4
SIDE = 4
SCALE = 192 ** -0.5
LOG2E = 1.4426950408889634
NT = (((1,), (1,)), ((), ()))
MESH = pl.DeviceIdType.MESH
F32 = jnp.float32
BF16 = jnp.bfloat16


def place():
    me = lax.axis_index("ctx")
    return me, me // SIDE, me % SIDE


def ctx_at(x, y):
    return (x % SIDE) * SIDE + y % SIDE


def remote(src, dst, send, recv, device):
    return pltpu.make_async_remote_copy(
        src_ref=src, dst_ref=dst, send_sem=send, recv_sem=recv, device_id=device, device_id_type=MESH
    )


def greet(devices):
    barrier = pltpu.get_barrier_semaphore()
    for device in devices:
        pl.semaphore_signal(barrier, inc=1, device_id=device, device_id_type=MESH)
    pl.semaphore_wait(barrier, len(devices))


def line_peers(x, y):
    return [{"ctx": ctx_at(x + d, y)} for d in (1, 2, 3)] + [{"ctx": ctx_at(x, y + d)} for d in (1, 2, 3)]


def plane_gather(every, x, y, send, recv):
    top, low = pl.ds(0, HALF), pl.ds(HALF, HALF)

    def copy(bx, by, rows, k, dx, dy):
        piece = every.at[ctx_at(bx, by), rows]
        return remote(piece, piece, send.at[k], recv.at[k], {"ctx": ctx_at(x + dx, y + dy)})

    started = []

    def start(*args):
        c = copy(*args)
        c.start()
        started.append(c)

    for d in (1, 3, 2):
        start(x, y, top, d - 1, d, 0)
        start(x, y, low, 3 + d - 1, 0, d)
    for j in (0, 1, 3, 2):
        if j > 0:
            copy(x - j, y, top, j - 1, j, 0).wait_recv()
            copy(x, y - j, low, 3 + j - 1, 0, j).wait_recv()
        for d in (1, 3, 2):
            start(x - j, y, top, 6 + 3 * j + d - 1, 0, d)
            start(x, y - j, low, 18 + 3 * j + d - 1, d, 0)
    for j in (0, 1, 3, 2):
        for d in (1, 3, 2):
            copy(x - j, y - d, top, 6 + 3 * j + d - 1, 0, d).wait_recv()
            copy(x - d, y - j, low, 18 + 3 * j + d - 1, d, 0).wait_recv()
    for c in started:
        c.wait_send()


def gather_kernel(lat_ref, every_ref, send, recv, own_sem):
    me, x, y = place()
    own = pltpu.make_async_copy(lat_ref.at[0], every_ref.at[me], own_sem)
    own.start()
    greet(line_peers(x, y))
    own.wait()
    plane_gather(every_ref, x, y, send, recv)


def gather_latents(latents):
    return pl.pallas_call(
        gather_kernel,
        out_shape=jax.ShapeDtypeStruct((16, W, TOK), BF16),
        in_specs=[pl.BlockSpec(memory_space=pl.ANY)],
        out_specs=pl.BlockSpec(memory_space=pl.ANY),
        scratch_shapes=[pltpu.SemaphoreType.DMA((30,)), pltpu.SemaphoreType.DMA((30,)), pltpu.SemaphoreType.DMA],
        compiler_params=pltpu.CompilerParams(collective_id=0, has_side_effects=True),
        name="gather_latents",
    )(latents)


def attn_kernel(heads, sub, lst, k0, k1, k2, k3, qt_ref, do_ref, own_ref, parts_ref, acc, k_scr, d_scr):
    step = pl.program_id(0)

    @pl.when(step == 0)
    def _():
        for e, k_ref in enumerate((k0, k1, k2, k3)):
            k_scr[e * TOK : (e + 1) * TOK, :] = k_ref[0].T
        acc[...] = jnp.zeros_like(acc)

    tg = 256 // heads
    ri = lax.broadcasted_iota(jnp.int32, (256, 256), 0)
    ci = lax.broadcasted_iota(jnp.int32, (256, 256), 1)
    perm = jnp.where((ri // tg == ci % heads) & (ri % tg == ci // heads), 1.0, 0.0).astype(BF16)
    for g in range(TOK // tg):
        rows = do_ref[g * tg : (g + 1) * tg].reshape(256, R)
        moved = jnp.dot(perm, rows, preferred_element_type=F32)
        d_scr[:, g * tg : (g + 1) * tg, :] = moved.astype(BF16).reshape(heads, tg, R)
    key_at = lax.broadcasted_iota(jnp.int32, (TOK, TOK), 0)
    tok_at = lax.broadcasted_iota(jnp.int32, (TOK, TOK), 1)
    causal = jnp.concatenate([key_at <= tok_at] * sub, axis=1)
    away = [None] + [jnp.where(lst[e] >= 0, 0.0, jnp.inf) for e in range(1, SLOTS)]
    c = SCALE * LOG2E
    keys = k_scr[...]
    for j in range(heads // sub):
        qt = jnp.concatenate([qt_ref[j * sub + i] for i in range(sub)], axis=1)
        d = d_scr[j * sub : (j + 1) * sub].reshape(sub * TOK, R)
        s = jnp.dot(keys, qt, preferred_element_type=F32)
        dp = lax.dot_general(keys[:, :R], d, NT, preferred_element_type=F32)
        ss = [s[e * TOK : (e + 1) * TOK] for e in range(SLOTS)]
        ss[0] = jnp.where(causal, ss[0], -jnp.inf)
        top = jnp.max(ss[0], axis=0, keepdims=True)
        for e in range(1, SLOTS):
            top = jnp.maximum(top, jnp.max(ss[e], axis=0, keepdims=True) - away[e])
        mc = top * c
        p = jnp.concatenate(
            [jnp.exp2(ss[e] * c - (mc if e == 0 else mc + away[e])) for e in range(SLOTS)], axis=0
        )
        inv = 1.0 / jnp.sum(p, axis=0, keepdims=True)
        delta = jnp.sum(p * dp, axis=0, keepdims=True) * inv
        probs = p * inv
        ds = (probs * (dp - delta)).astype(BF16)
        pb = probs.astype(BF16)
        kg = lax.dot_general(ds, qt, NT, preferred_element_type=F32) * SCALE
        vg = jnp.dot(pb, d, preferred_element_type=F32)
        acc[:, :R] += kg[:, :R] + vg
        acc[:, R:] += kg[:, R:]

    @pl.when(step == pl.num_programs(0) - 1)
    def _():
        own_ref[...] = acc[:TOK].T
        for e in range(1, SLOTS):
            parts_ref[e - 1] = acc[e * TOK : (e + 1) * TOK].T.astype(BF16)


def attention(row, every, qt, do, heads=16, sub=4):
    n_heads = qt.shape[0]
    spec = lambda e: pl.BlockSpec((1, W, TOK), lambda g, l: (jnp.maximum(l[e], 0), 0, 0))
    return pl.pallas_call(
        functools.partial(attn_kernel, heads, sub),
        grid_spec=pltpu.PrefetchScalarGridSpec(
            num_scalar_prefetch=1,
            grid=(n_heads // heads,),
            in_specs=[spec(e) for e in range(SLOTS)]
            + [
                pl.BlockSpec((heads, W, TOK), lambda g, l: (g, 0, 0)),
                pl.BlockSpec((TOK, heads, R), lambda g, l: (0, g, 0)),
            ],
            out_specs=[
                pl.BlockSpec((W, TOK), lambda g, l: (0, 0)),
                pl.BlockSpec((SLOTS - 1, W, TOK), lambda g, l: (0, 0, 0)),
            ],
            scratch_shapes=[
                pltpu.VMEM((SLOTS * TOK, W), F32),
                pltpu.VMEM((SLOTS * TOK, W), BF16),
                pltpu.VMEM((heads, TOK, R), BF16),
            ],
        ),
        out_shape=[
            jax.ShapeDtypeStruct((W, TOK), F32),
            jax.ShapeDtypeStruct((SLOTS - 1, W, TOK), BF16),
        ],
        compiler_params=pltpu.CompilerParams(vmem_limit_bytes=56 * 2**20),
        cost_estimate=pl.CostEstimate(flops=22 * 10**9, bytes_accessed=20 * 10**6, transcendentals=4 * 10**6),
        name="attention",
    )(row, every, every, every, every, qt, do)


def tail_kernel(
    lst, own_ref, parts_ref, xt_ref, lat_ref, w_ref,
    raw, mid, back, near, every, pieces, arrived, total, totals,
    raw_s, raw_r, mid_s, mid_r, near_s, near_r, all_s, all_r, dp_s, dp_r, sum_s, sum_r,
):
    me, x, y = place()
    dp = lax.axis_index("dp")
    n_dp = pieces.shape[0]
    greet(
        line_peers(x, y)
        + [{"ctx": (me + 1) % 16}, {"ctx": (me + 15) % 16}]
        + [{"dp": (dp + d) % n_dp} for d in range(1, n_dp)]
    )
    halves = (pl.ds(0, HALF), pl.ds(HALF, HALF))
    started = []

    def start(c):
        c.start()
        started.append(c)

    def raw_copy(half, d):
        return remote(
            parts_ref.at[pl.ds(1, 2), halves[half]],
            raw.at[half, d - 1],
            raw_s.at[half, d - 1],
            raw_r.at[half, d - 1],
            {"ctx": ctx_at(x, y + d) if half == 0 else ctx_at(x + d, y)},
        )

    for d in (1, 3, 2):
        for half in (0, 1):
            start(raw_copy(half, d))
    near_copy = remote(parts_ref.at[0], near, near_s, near_r, {"ctx": (me + 15) % 16})
    start(near_copy)

    def mid_copy(half, d):
        return remote(
            mid.at[half, d - 1],
            back.at[half, d - 1],
            mid_s.at[half, d - 1],
            mid_r.at[half, d - 1],
            {"ctx": ctx_at(x + d, y) if half == 0 else ctx_at(x, y + d)},
        )

    kept = []
    for half in (0, 1):
        found = []
        for d in range(SIDE):
            src = ctx_at(x, y - d) if half == 0 else ctx_at(x - d, y)
            if d > 0:
                raw_copy(half, d).wait_recv()
            for e in range(2):
                part = parts_ref[1 + e, halves[half]] if d == 0 else raw[half, d - 1, e]
                found.append((lst[src, 2 + e], part.astype(F32)))
        for d in (1, 3, 2, 0):
            target = ctx_at(x + d, y) if half == 0 else ctx_at(x, y + d)
            added = None
            for entry, part in found:
                term = part * jnp.where(entry == target, 1.0, 0.0)
                added = term if added is None else added + term
            if d == 0:
                kept.append(added)
            else:
                mid[half, d - 1] = added.astype(BF16)
                start(mid_copy(half, d))

    near_copy.wait_recv()
    has_next = jnp.where(me < 15, 1.0, 0.0)
    for half in (0, 1):
        for d in (1, 2, 3):
            mid_copy(half, d).wait_recv()
        rows = halves[half]
        result = own_ref[rows] + near[rows].astype(F32) * has_next + kept[half]
        for d in (1, 2, 3):
            result += back[half, d - 1].astype(F32)
        lat_ref[rows] = result
        every[me, rows] = result.astype(BF16)

    plane_gather(every, x, y, all_s, all_r)

    weight = None
    for b in range(0, 16, 4):
        xt = jnp.concatenate([xt_ref[b + i] for i in range(4)], axis=1)
        gt = jnp.concatenate([every[b + i] for i in range(4)], axis=1)
        term = lax.dot_general(xt, gt, NT, preferred_element_type=F32)
        weight = term if weight is None else weight + term
    rows = weight.shape[0] // n_dp
    for i in range(n_dp):
        pieces[i, :rows] = weight[i * rows : (i + 1) * rows].astype(BF16)
        pieces[i, rows:] = jnp.zeros((pieces.shape[1] - rows, W), BF16)

    def dp_copy(d):
        to = (dp + d) % n_dp
        return remote(pieces.at[to], arrived.at[d - 1], dp_s.at[d - 1], dp_r.at[d - 1], {"dp": to})

    def sum_copy(d, owner):
        return remote(total, totals.at[owner], sum_s.at[d - 1], sum_r.at[d - 1], {"dp": (dp + d) % n_dp})

    for d in range(1, n_dp):
        start(dp_copy(d))
    added = pieces[dp].astype(F32)
    for d in range(1, n_dp):
        dp_copy(d).wait_recv()
        added += arrived[d - 1].astype(F32)
    total[...] = added.astype(BF16)
    for d in range(1, n_dp):
        start(sum_copy(d, dp))
    totals[dp] = total[...]
    for d in range(1, n_dp):
        sum_copy(d, (dp + n_dp - d) % n_dp).wait_recv()
    for i in range(n_dp):
        w_ref[i * rows : (i + 1) * rows] = totals[i].astype(F32)[:rows]
    for c in started:
        c.wait_send()


def tail(rows_list, own, parts, xt, n_dp):
    cols = xt.shape[1]
    vmem = pl.BlockSpec(memory_space=pltpu.VMEM)
    pad = (cols // n_dp + 15) // 16 * 16
    dma = pltpu.SemaphoreType.DMA
    return pl.pallas_call(
        tail_kernel,
        out_shape=[jax.ShapeDtypeStruct((W, TOK), F32), jax.ShapeDtypeStruct((cols, W), F32)],
        in_specs=[pl.BlockSpec(memory_space=pltpu.SMEM), vmem, vmem, vmem],
        out_specs=[vmem, vmem],
        scratch_shapes=[
            pltpu.VMEM((2, 3, 2, HALF, TOK), BF16),
            pltpu.VMEM((2, 3, HALF, TOK), BF16),
            pltpu.VMEM((2, 3, HALF, TOK), BF16),
            pltpu.VMEM((W, TOK), BF16),
            pltpu.VMEM((16, W, TOK), BF16),
            pltpu.VMEM((n_dp, pad, W), BF16),
            pltpu.VMEM((n_dp - 1, pad, W), BF16),
            pltpu.VMEM((pad, W), BF16),
            pltpu.VMEM((n_dp, pad, W), BF16),
            dma((2, 3)), dma((2, 3)), dma((2, 3)), dma((2, 3)), dma, dma,
            dma((30,)), dma((30,)), dma((n_dp - 1,)), dma((n_dp - 1,)), dma((n_dp - 1,)), dma((n_dp - 1,)),
        ],
        compiler_params=pltpu.CompilerParams(
            collective_id=1, has_side_effects=True, vmem_limit_bytes=48 * 2**20
        ),
        name="tail",
    )(rows_list, own, parts, xt)


def per_device(queries, latents, out_grad, layer_input, block_list):
    own_block = lax.axis_index("ctx")
    n_dp = lax.axis_size("dp")
    row_list = lax.dynamic_index_in_dim(block_list[0], own_block, 0, keepdims=False)
    every = gather_latents(latents.transpose(0, 2, 1))
    inputs_t = layer_input[0].T.reshape(16, -1, TOK)
    xt = lax.all_to_all(inputs_t, "ctx", 0, 0, tiled=True)
    own, parts = attention(row_list, every, queries[0].transpose(1, 2, 0), out_grad[0])
    lat_t, weight_grad = tail(block_list[0], own, parts, xt, n_dp)
    return (lat_t.T[None], weight_grad)


def solution(mesh):
    placed = (
        P("dp", "ctx", None, None),
        P("dp", "ctx", None),
        P("dp", "ctx", None, None),
        P("dp", "ctx", None),
        P("dp", None, None),
    )
    return jax.shard_map(
        per_device,
        mesh=mesh,
        in_specs=placed,
        out_specs=(P("dp", "ctx", None), P("ctx", None)),
        check_vma=False,
    )
```

```python
import jax
import jax.numpy as jnp
from jax import lax
from jax.experimental import pallas as pl
from jax.experimental.pallas import tpu as pltpu
from jax.sharding import PartitionSpec as P

R = 512
W = 576
HALF = 288
TOK = 128
SLOTS = 4
SIDE = 4
HEADS = 16
SUB = 4
SCALE = 192 ** -0.5
LOG2E = 1.4426950408889634
NT = (((1,), (1,)), ((), ()))
MESH = pl.DeviceIdType.MESH
F32 = jnp.float32
BF16 = jnp.bfloat16
TOP, LOW = pl.ds(0, HALF), pl.ds(HALF, HALF)


def place():
    me = lax.axis_index("ctx")
    return me, me // SIDE, me % SIDE


def ctx_at(x, y):
    return (x % SIDE) * SIDE + y % SIDE


def remote(src, dst, send, recv, device):
    return pltpu.make_async_remote_copy(
        src_ref=src, dst_ref=dst, send_sem=send, recv_sem=recv, device_id=device, device_id_type=MESH
    )


def greet(devices):
    barrier = pltpu.get_barrier_semaphore()
    for device in devices:
        pl.semaphore_signal(barrier, inc=1, device_id=device, device_id_type=MESH)
    pl.semaphore_wait(barrier, len(devices))


def line_peers(x, y):
    return [{"ctx": ctx_at(x + d, y)} for d in (1, 2, 3)] + [{"ctx": ctx_at(x, y + d)} for d in (1, 2, 3)]


class Gather:
    def __init__(self, every, x, y, send, recv, started):
        self.every, self.x, self.y, self.send, self.recv, self.started = every, x, y, send, recv, started

    def copy(self, bx, by, rows, k, dx, dy):
        piece = self.every.at[ctx_at(bx, by), rows]
        device = {"ctx": ctx_at(self.x + dx, self.y + dy)}
        return remote(piece, piece, self.send.at[k], self.recv.at[k], device)

    def start(self, *args):
        c = self.copy(*args)
        c.start()
        self.started.append(c)

    def first(self):
        x, y = self.x, self.y
        for d in (1, 3, 2):
            self.start(x, y, TOP, d - 1, d, 0)
            self.start(x, y, LOW, 3 + d - 1, 0, d)

    def forward(self, j):
        x, y = self.x, self.y
        if j > 0:
            self.copy(x - j, y, TOP, j - 1, j, 0).wait_recv()
            self.copy(x, y - j, LOW, 3 + j - 1, 0, j).wait_recv()
        for d in (1, 3, 2):
            self.start(x - j, y, TOP, 6 + 3 * j + d - 1, 0, d)
            self.start(x, y - j, LOW, 18 + 3 * j + d - 1, d, 0)

    def finish(self):
        x, y = self.x, self.y
        for j in range(SIDE):
            for d in (1, 2, 3):
                self.copy(x - j, y - d, TOP, 6 + 3 * j + d - 1, 0, d).wait_recv()
                self.copy(x - d, y - j, LOW, 18 + 3 * j + d - 1, d, 0).wait_recv()


def kernel(
    lst, lat, qt, do, inp, lat_ref, w_ref,
    q_v, stage, d_v, every, prev, k_v, s_v, dp_v, acc, parts, raw, mid, back, near, gbuf, xa, xt,
    cs0, cs1, cr0, cr1, ys0, ys1, yr0, yr1, zr0, zr1, fin0, fin1,
    q_s, do_s, own_s, all_s, all_r, prev_s, prev_r, x_s, x_r, xo_s, raw_s, raw_r, mid_s, mid_r, near_s, near_r,
    g_s, g_r, c_s, c_r, y_s, y_r, z_s, z_r, f_s, f_r,
):
    me, x, y = place()
    dp = lax.axis_index("dp")
    n_dp = lax.axis_size("dp")
    core, z = dp % 2, dp // 2
    twin = {"dp": dp + 1 - 2 * core}
    after, before = {"ctx": (me + 1) % 16}, {"ctx": (me + 15) % 16}
    n_heads = q_v.shape[0]
    steps = n_heads // HEADS
    quarter = xa.shape[2]
    started = []

    def start(c):
        c.start()
        started.append(c)

    def do_load(i):
        return pltpu.make_async_copy(do.at[:, pl.ds(i * HEADS, HEADS)], stage.at[i % 2], do_s.at[i % 2])

    def q_load(i):
        part = pl.ds(i * HEADS, HEADS)
        return pltpu.make_async_copy(qt.at[part], q_v.at[part], q_s.at[i])

    own_load = pltpu.make_async_copy(lat.at[0], every.at[me], own_s)
    own_load.start()
    do_load(0).start()
    q_load(0).start()
    do_load(1).start()
    for i in range(1, steps):
        q_load(i).start()
    x_own = pltpu.make_async_copy(
        inp.at[:, pl.ds(pl.multiple_of(x * quarter, 128), quarter)], xa.at[0], xo_s
    )
    greet(
        line_peers(x, y) + [after, before, twin] + [{"dp": (dp + 2 * d) % n_dp} for d in range(1, n_dp // 2)]
    )
    own_load.wait()
    prev_copy = remote(every.at[me], prev, prev_s, prev_r, after)
    start(prev_copy)
    gather = Gather(every, x, y, all_s, all_r, started)
    gather.first()
    x_own.start()

    k_v[:TOK] = every[me].T
    prev_copy.wait_recv()
    k_v[TOK : 2 * TOK] = prev[...].T
    gather.forward(0)

    def columns(at):
        return (
            jnp.concatenate([q_v[at * SUB + i] for i in range(SUB)], axis=1),
            d_v[pl.ds(at * SUB, SUB)].reshape(SUB * TOK, R),
        )

    def products(keys, qc, dc):
        return (
            jnp.dot(keys, qc, preferred_element_type=F32),
            lax.dot_general(keys[:, :R], dc, NT, preferred_element_type=F32),
        )

    per = HEADS // SUB
    for i in range(steps):
        do_load(i).wait()
        q_load(i).wait()
        d_v[i * HEADS : (i + 1) * HEADS] = jnp.swapaxes(stage[i % 2], 0, 1)
        if i + 2 < steps:
            do_load(i + 2).start()

        window = k_v[: 2 * TOK]
        for k in range(per):
            at = i * per + k
            s_v[at], dp_v[at] = products(window, *columns(at))
        if i < 2:
            for j in ((1, 3), (2,))[i]:
                gather.forward(j)
    gather.finish()

    def x_copy(d):
        to = (x + d) % SIDE
        return remote(
            inp.at[:, pl.ds(pl.multiple_of(to * quarter, 128), quarter)],
            xa.at[d], x_s.at[d - 1], x_r.at[d - 1], {"ctx": ctx_at(x + d, y)},
        )

    for d in (1, 3, 2):
        start(x_copy(d))

    for e in (2, 3):
        k_v[e * TOK : (e + 1) * TOK] = every[jnp.maximum(lst[me, e], 0)].T
    acc[...] = jnp.zeros_like(acc)
    key_at = lax.broadcasted_iota(jnp.int32, (TOK, TOK), 0)
    tok_at = lax.broadcasted_iota(jnp.int32, (TOK, TOK), 1)
    causal = jnp.concatenate([key_at <= tok_at] * SUB, axis=1)
    away = [None] + [jnp.where(lst[me, e] >= 0, 0.0, jnp.inf) for e in range(1, SLOTS)]
    c = SCALE * LOG2E

    def softmax(at):
        qc, dc = columns(at)
        s_far, dp_far = products(k_v[2 * TOK :], qc, dc)
        ss = [s_v[at, :TOK], s_v[at, TOK:], s_far[:TOK], s_far[TOK:]]
        dprob = jnp.concatenate([dp_v[at], dp_far], axis=0)
        ss[0] = jnp.where(causal, ss[0], -jnp.inf)
        top = jnp.max(ss[0], axis=0, keepdims=True)
        for e in range(1, SLOTS):
            top = jnp.maximum(top, jnp.max(ss[e], axis=0, keepdims=True) - away[e])
        mc = top * c
        p = jnp.concatenate(
            [jnp.exp2(ss[e] * c - (mc if e == 0 else mc + away[e])) for e in range(SLOTS)], axis=0
        )
        inv = 1.0 / jnp.sum(p, axis=0, keepdims=True)
        delta = jnp.sum(p * dprob, axis=0, keepdims=True) * inv
        probs = p * inv
        return qc, dc, probs.astype(BF16), (probs * (dprob - delta)).astype(BF16)

    def grads(qc, dc, pb, ds):
        kg = lax.dot_general(ds, qc, NT, preferred_element_type=F32) * SCALE
        vg = jnp.dot(pb, dc, preferred_element_type=F32)
        acc[:, :R] += kg[:, :R] + vg
        acc[:, R:] += kg[:, R:]

    def attend(i, carry):
        held = None
        for k in range(per):
            fresh = softmax(i * per + k)
            if held is not None:
                grads(*held)
            held = fresh
        grads(*held)
        return carry

    lax.fori_loop(0, steps, attend, 0)

    halves = (TOP, LOW)

    def raw_copy(half, d):
        return remote(
            parts.at[pl.ds(1, 2), halves[half]], raw.at[half, d - 1], raw_s.at[half, d - 1], raw_r.at[half, d - 1],
            {"ctx": ctx_at(x, y + d) if half == 0 else ctx_at(x + d, y)},
        )

    for e in (2, 3):
        parts[e - 1] = acc[e * TOK : (e + 1) * TOK].T.astype(BF16)
    for d in (1, 3, 2):
        for half in (0, 1):
            start(raw_copy(half, d))
    parts[0] = acc[TOK : 2 * TOK].T.astype(BF16)
    near_copy = remote(parts.at[0], near, near_s, near_r, before)
    start(near_copy)

    x_own.wait()
    for d in range(SIDE):
        if d > 0:
            x_copy(d).wait_recv()
        xt[:, d * TOK : (d + 1) * TOK] = xa[d].T
    lat_ref[...] = acc[:TOK].T

    def mid_copy(half, d):
        return remote(
            mid.at[half, d - 1], back.at[half, d - 1], mid_s.at[half, d - 1], mid_r.at[half, d - 1],
            {"ctx": ctx_at(x + d, y) if half == 0 else ctx_at(x, y + d)},
        )

    for half in (0, 1):
        found = []
        for d in range(SIDE):
            src = ctx_at(x, y - d) if half == 0 else ctx_at(x - d, y)
            if d > 0:
                raw_copy(half, d).wait_recv()
            for e in range(2):
                part = parts[1 + e, halves[half]] if d == 0 else raw[half, d - 1, e]
                found.append((lst[src, 2 + e], part.astype(F32)))
        for d in (1, 3, 2, 0):
            target = ctx_at(x + d, y) if half == 0 else ctx_at(x, y + d)
            added = None
            for entry, part in found:
                term = part * jnp.where(entry == target, 1.0, 0.0)
                added = term if added is None else added + term
            if d == 0:
                lat_ref[halves[half]] += added
            else:
                mid[half, d - 1] = added.astype(BF16)
                start(mid_copy(half, d))

    near_copy.wait_recv()
    has_next = jnp.where(me < 15, 1.0, 0.0)
    for half in (0, 1):
        rows = halves[half]
        result = lat_ref[rows] + near[rows].astype(F32) * has_next
        for d in (1, 2, 3):
            mid_copy(half, d).wait_recv()
            result += back[half, d - 1].astype(F32)
        lat_ref[rows] = result
        gbuf[0, rows] = result.astype(BF16)

    chunks = ((0, 256), (256, W - 256))
    cs, cr, ys, yr = (cs0, cs1), (cr0, cr1), (ys0, ys1), (yr0, yr1)
    zr, fin = (zr0, zr1), (fin0, fin1)

    def g_copy(ch, d):
        rows = pl.ds(*chunks[ch])
        return remote(
            gbuf.at[0, rows], gbuf.at[d, rows], g_s.at[ch, d - 1], g_r.at[ch, d - 1], {"ctx": ctx_at(x + d, y)}
        )

    def c_copy(ch):
        return remote(cs[ch], cr[ch], c_s.at[ch], c_r.at[ch], twin)

    def y_copy(ch, d):
        to = (y + d) % SIDE
        return remote(ys[ch].at[to], yr[ch].at[d - 1], y_s.at[ch, d - 1], y_r.at[ch, d - 1], {"ctx": ctx_at(x, to)})

    def z_copy(ch, d, owner):
        piece = zr[ch].at[owner]
        return remote(piece, piece, z_s.at[ch, d - 1], z_r.at[ch, d - 1], {"dp": (dp + 2 * d) % n_dp})

    def f_copy(ch, owner):
        piece = fin[ch].at[owner]
        return remote(piece, piece, f_s.at[ch], f_r.at[ch], twin)

    part = cs0.shape[1]

    def slot(ch, row, half):
        return s_v.at[(ch * SIDE + row) * 2 + half, pl.ds(0, part), pl.ds(0, chunks[ch][1])]

    n_z = n_dp // 2
    for ch in (0, 1):
        for d in (1, 3, 2):
            start(g_copy(ch, d))
    for ch in (0, 1):
        for d in (1, 2, 3):
            g_copy(ch, d).wait_recv()
        rows = pl.ds(*chunks[ch])
        gt = jnp.concatenate([gbuf[d, rows] for d in range(SIDE)], axis=1)
        weight = lax.dot_general(xt[...], gt, NT, preferred_element_type=F32)
        for i in range(2 * SIDE):
            slot(ch, i // 2, i % 2)[...] = weight[i * part : (i + 1) * part]
        for i in range(SIDE):
            cs[ch][i] = slot(ch, i, 1 - core)[...].astype(BF16)
        start(c_copy(ch))
    for ch in (0, 1):
        c_copy(ch).wait_recv()
        for i in range(SIDE):
            both = slot(ch, i, core)[...] + cr[ch][i].astype(F32)
            slot(ch, i, core)[...] = both
            ys[ch][i] = both.astype(BF16)
        for d in (1, 3, 2):
            start(y_copy(ch, d))
    for ch in (0, 1):
        added = slot(ch, y, core)[...]
        for d in (1, 2, 3):
            y_copy(ch, d).wait_recv()
            added += yr[ch][d - 1].astype(F32)
        zr[ch][z] = added.astype(BF16)
        for d in range(1, n_z):
            start(z_copy(ch, d, z))
    for ch in (0, 1):
        for d in range(1, n_z):
            z_copy(ch, d, (z + n_z - d) % n_z).wait_recv()
        added = zr[ch][0].astype(F32)
        for i in range(1, n_z):
            added += zr[ch][i].astype(F32)
        fin[ch][core] = added
        start(f_copy(ch, core))
    for ch in (0, 1):
        f_copy(ch, 1 - core).wait_recv()
        first, count = chunks[ch]
        for i in (0, 1):
            half_rows = fin[ch].shape[1]
            w_ref[i * half_rows : (i + 1) * half_rows, first : first + count] = fin[ch][i]
    for c in started:
        c.wait_send()


def per_device(queries, latents, out_grad, layer_input, block_list):
    n_dp = lax.axis_size("dp")
    n_z = n_dp // 2
    n_heads = queries.shape[2]
    cols = layer_input.shape[2] // 16
    vmem = pl.BlockSpec(memory_space=pltpu.VMEM)
    hbm = pl.BlockSpec(memory_space=pl.ANY)
    dma = pltpu.SemaphoreType.DMA
    v = pltpu.VMEM
    n0, n1 = 256, W - 256
    part = cols // 2
    lat_t, weight_grad = pl.pallas_call(
        kernel,
        out_shape=[jax.ShapeDtypeStruct((W, TOK), F32), jax.ShapeDtypeStruct((cols, W), F32)],
        in_specs=[pl.BlockSpec(memory_space=pltpu.SMEM), hbm, hbm, hbm, hbm],
        out_specs=[vmem, vmem],
        scratch_shapes=[
            v((n_heads, W, TOK), BF16),
            v((2, TOK, HEADS, R), BF16),
            v((n_heads, TOK, R), BF16),
            v((16, W, TOK), BF16),
            v((W, TOK), BF16),
            v((SLOTS * TOK, W), BF16),
            v((n_heads // SUB, 2 * TOK, SUB * TOK), F32),
            v((n_heads // SUB, 2 * TOK, SUB * TOK), F32),
            v((SLOTS * TOK, W), F32),
            v((3, W, TOK), BF16),
            v((2, 3, 2, HALF, TOK), BF16),
            v((2, 3, HALF, TOK), BF16),
            v((2, 3, HALF, TOK), BF16),
            v((W, TOK), BF16),
            v((SIDE, W, TOK), BF16),
            v((SIDE, TOK, SIDE * cols), BF16),
            v((SIDE * cols, SIDE * TOK), BF16),
            v((SIDE, part, n0), BF16), v((SIDE, part, n1), BF16),
            v((SIDE, part, n0), BF16), v((SIDE, part, n1), BF16),
            v((SIDE, part, n0), BF16), v((SIDE, part, n1), BF16),
            v((3, part, n0), BF16), v((3, part, n1), BF16),
            v((n_z, part, n0), BF16), v((n_z, part, n1), BF16),
            v((2, part, n0), F32), v((2, part, n1), F32),
            dma((n_heads // HEADS,)), dma((2,)), dma, dma((30,)), dma((30,)), dma, dma,
            dma((3,)), dma((3,)), dma, dma((2, 3)), dma((2, 3)), dma((2, 3)), dma((2, 3)), dma, dma,
            dma((2, 3)), dma((2, 3)), dma((2,)), dma((2,)), dma((2, 3)), dma((2, 3)),
            dma((2, n_z - 1)), dma((2, n_z - 1)), dma((2,)), dma((2,)),
        ],
        compiler_params=pltpu.CompilerParams(
            collective_id=0, has_side_effects=True, vmem_limit_bytes=60 * 2**20
        ),
        name="attention_backward",
    )(
        block_list[0],
        latents.transpose(0, 2, 1),
        queries[0].transpose(1, 2, 0),
        out_grad[0],
        layer_input[0],
    )
    return (lat_t.T[None], weight_grad)


def solution(mesh):
    placed = (
        P("dp", "ctx", None, None),
        P("dp", "ctx", None),
        P("dp", "ctx", None, None),
        P("dp", "ctx", None),
        P("dp", None, None),
    )
    return jax.shard_map(
        per_device,
        mesh=mesh,
        in_specs=placed,
        out_specs=(P("dp", "ctx", None), P("ctx", None)),
        check_vma=False,
    )
```

```python
import jax
import jax.numpy as jnp
from jax import lax
from jax.experimental import pallas as pl
from jax.experimental.pallas import tpu as pltpu
from jax.sharding import PartitionSpec as P

R = 512
W = 576
HALF = 288
TOK = 128
SLOTS = 4
SIDE = 4
HEADS = 16
SUB = 4
SPANS = ((0, 128), (128, 192), (320, 128), (448, 128))
SCALE = 192 ** -0.5
LOG2E = 1.4426950408889634
NT = (((1,), (1,)), ((), ()))
MESH = pl.DeviceIdType.MESH
F32 = jnp.float32
BF16 = jnp.bfloat16
TOP, LOW = pl.ds(0, HALF), pl.ds(HALF, HALF)


def place():
    me = lax.axis_index("ctx")
    return me, me // SIDE, me % SIDE


def ctx_at(x, y):
    return (x % SIDE) * SIDE + y % SIDE


def remote(src, dst, send, recv, device):
    return pltpu.make_async_remote_copy(
        src_ref=src, dst_ref=dst, send_sem=send, recv_sem=recv, device_id=device, device_id_type=MESH
    )


def greet(devices):
    barrier = pltpu.get_barrier_semaphore()
    for device in devices:
        pl.semaphore_signal(barrier, inc=1, device_id=device, device_id_type=MESH)
    pl.semaphore_wait(barrier, len(devices))


def line_peers(x, y):
    return [{"ctx": ctx_at(x + d, y)} for d in (1, 2, 3)] + [{"ctx": ctx_at(x, y + d)} for d in (1, 2, 3)]


def kernel(
    lst, lat, qt, do, inp, lat_ref, w_ref,
    q_v, stage, d_v, line, sel, got, prev, k_v, s_v, dp_v, acc, parts, raw, mid, back, near, gbuf, xa, xt,
    cs, cr, ys, yr, zr, fin,
    q_s, do_s, own_s, line_s, line_r, sel_s, sel_r, prev_s, prev_r, x_s, x_r, xo_s, raw_s, raw_r, mid_s, mid_r, near_s, near_r,
    g_s, g_r, c_s, c_r, y_s, y_r, z_s, z_r, f_s, f_r,
):
    me, x, y = place()
    dp = lax.axis_index("dp")
    n_dp = lax.axis_size("dp")
    core, z = dp % 2, dp // 2
    twin = {"dp": dp + 1 - 2 * core}
    after, before = {"ctx": (me + 1) % 16}, {"ctx": (me + 15) % 16}
    n_heads = q_v.shape[0]
    steps = n_heads // HEADS
    quarter = xa.shape[2]
    started = []

    def start(c):
        c.start()
        started.append(c)

    def do_load(i):
        return pltpu.make_async_copy(do.at[:, pl.ds(i * HEADS, HEADS)], stage.at[i % 2], do_s.at[i % 2])

    def q_load(i):
        part = pl.ds(i * HEADS, HEADS)
        return pltpu.make_async_copy(qt.at[part], q_v.at[part], q_s.at[i])

    halves = (TOP, LOW)
    chunks = ((0, 256), (256, W - 256))
    mine = (line.at[0, x], line.at[1, y])
    own_loads = [pltpu.make_async_copy(lat.at[0, halves[h]], mine[h], own_s.at[h]) for h in (0, 1)]
    for load in own_loads:
        load.start()
    do_load(0).start()
    q_load(0).start()
    do_load(1).start()
    for i in range(1, steps):
        q_load(i).start()
    x_own = pltpu.make_async_copy(
        inp.at[:, pl.ds(pl.multiple_of(x * quarter, 128), quarter)], xa.at[0], xo_s
    )
    greet(
        line_peers(x, y) + [after, before, twin] + [{"dp": (dp + 2 * d) % n_dp} for d in range(1, n_dp // 2)]
    )
    for load in own_loads:
        load.wait()

    def along(half, d):
        return {"ctx": ctx_at(x + d, y) if half == 0 else ctx_at(x, y + d)}

    def across(half, d):
        return along(1 - half, d)

    def line_copy(half, d):
        return remote(mine[half], mine[half], line_s.at[half, d - 1], line_r.at[half, d - 1], along(half, d))

    def line_wait(half, d):
        slot = line.at[0, (x + SIDE - d) % SIDE] if half == 0 else line.at[1, (y + SIDE - d) % SIDE]
        remote(slot, slot, line_s.at[half, d - 1], line_r.at[half, d - 1], along(half, d)).wait_recv()

    def prev_copy(half):
        return remote(mine[half], prev.at[half], prev_s.at[half], prev_r.at[half], after)

    start(prev_copy(0))

    @pl.when(y == SIDE - 1)
    def _():
        prev_copy(1).start()

    for d in (1, 3, 2):
        for half in (0, 1):
            start(line_copy(half, d))
    x_own.start()

    k_v[:TOK] = jnp.concatenate([line[0, x], line[1, y]], axis=0).T
    prev_copy(0).wait_recv()
    line_wait(1, 1)

    @pl.when(y == 0)
    def _():
        prev_copy(1).wait_recv()
        k_v[TOK : 2 * TOK] = jnp.concatenate([prev[0], prev[1]], axis=0).T

    @pl.when(y > 0)
    def _():
        k_v[TOK : 2 * TOK] = jnp.concatenate([prev[0], line[1, (y + SIDE - 1) % SIDE]], axis=0).T

    def listed(device, e):
        block = jnp.maximum(lst[2 + e, device], 0)
        return block >> 2, block & 3

    def sel_copy(half, d):
        return remote(
            sel.at[half, d - 1], got.at[half, d], sel_s.at[half, d - 1], sel_r.at[half, d - 1], across(half, d)
        )

    def pass_on():
        for half in (0, 1):
            for d in (1, 2, 3):
                if half == 0 or d > 1:
                    line_wait(half, d)
        for d in (1, 3, 2, 0):
            for half in (0, 1):
                for e in (0, 1):
                    wanted = listed(across(half, d)["ctx"], e)[half]
                    if d == 0:
                        got[half, 0, e] = line[half, wanted]
                    else:
                        sel[half, d - 1, e] = line[half, wanted]
                if d > 0:
                    start(sel_copy(half, d))

    def columns(at):
        return (
            jnp.concatenate([q_v[at * SUB + i] for i in range(SUB)], axis=1),
            d_v[pl.ds(at * SUB, SUB)].reshape(SUB * TOK, R),
        )

    def products(keys, qc, dc):
        return (
            jnp.dot(keys, qc, preferred_element_type=F32),
            lax.dot_general(keys[:, :R], dc, NT, preferred_element_type=F32),
        )

    per = HEADS // SUB
    for i in range(steps):
        do_load(i).wait()
        q_load(i).wait()
        d_v[i * HEADS : (i + 1) * HEADS] = jnp.swapaxes(stage[i % 2], 0, 1)
        if i + 2 < steps:
            do_load(i + 2).start()

        window = k_v[: 2 * TOK]
        for k in range(per):
            at = i * per + k
            s_v[at], dp_v[at] = products(window, *columns(at))
        if i == 0:
            pass_on()
    for half in (0, 1):
        for d in (1, 2, 3):
            sel_copy(half, d).wait_recv()

    def x_copy(d):
        to = (x + d) % SIDE
        return remote(
            inp.at[:, pl.ds(pl.multiple_of(to * quarter, 128), quarter)],
            xa.at[d], x_s.at[d - 1], x_r.at[d - 1], {"ctx": ctx_at(x + d, y)},
        )

    for d in (1, 3, 2):
        start(x_copy(d))

    for e in (0, 1):
        bx, by = listed(me, e)
        k_v[(2 + e) * TOK : (3 + e) * TOK] = jnp.concatenate(
            [got[0, (y - by) & 3, e], got[1, (x - bx) & 3, e]], axis=0
        ).T
    acc[...] = jnp.zeros_like(acc)
    key_at = lax.broadcasted_iota(jnp.int32, (TOK, TOK), 0)
    tok_at = lax.broadcasted_iota(jnp.int32, (TOK, TOK), 1)
    causal = jnp.concatenate([key_at <= tok_at] * SUB, axis=1)
    away = [None] + [jnp.where(lst[e, me] >= 0, 0.0, jnp.inf) for e in range(1, SLOTS)]
    c = SCALE * LOG2E

    def softmax(at):
        qc, dc = columns(at)
        s_far, dp_far = products(k_v[2 * TOK :], qc, dc)
        ss = [s_v[at, :TOK], s_v[at, TOK:], s_far[:TOK], s_far[TOK:]]
        dprob = jnp.concatenate([dp_v[at], dp_far], axis=0)
        ss[0] = jnp.where(causal, ss[0], -jnp.inf)
        top = jnp.max(ss[0], axis=0, keepdims=True)
        for e in range(1, SLOTS):
            top = jnp.maximum(top, jnp.max(ss[e], axis=0, keepdims=True) - away[e])
        mc = top * c
        p = jnp.concatenate(
            [jnp.exp2(ss[e] * c - (mc if e == 0 else mc + away[e])) for e in range(SLOTS)], axis=0
        )
        inv = 1.0 / jnp.sum(p, axis=0, keepdims=True)
        delta = jnp.sum(p * dprob, axis=0, keepdims=True) * inv
        probs = p * inv
        dscore = probs * (dprob - delta)
        s_v[at] = probs[: 2 * TOK]
        dp_v[at] = dscore[: 2 * TOK]
        return qc, dc, probs[2 * TOK :].astype(BF16), dscore[2 * TOK :].astype(BF16)

    def grads(qc, dc, pb, ds):
        kg = lax.dot_general(ds, qc, NT, preferred_element_type=F32) * SCALE
        vg = jnp.dot(pb, dc, preferred_element_type=F32)
        acc[2 * TOK :, :R] += kg[:, :R] + vg
        acc[2 * TOK :, R:] += kg[:, R:]

    def attend(i, carry):
        held = None
        for k in range(per):
            fresh = softmax(i * per + k)
            if held is not None:
                grads(*held)
            held = fresh
        grads(*held)
        return carry

    lax.fori_loop(0, steps, attend, 0)

    def window_grads(first, count):
        values = min(count, R - first)

        def step(i, carry):
            ats = [i * per + k for k in range(per)]
            ds = jnp.concatenate([dp_v[at].astype(BF16) for at in ats], axis=1)
            pb = jnp.concatenate([s_v[at].astype(BF16) for at in ats], axis=1)
            qc = jnp.concatenate([q_v[i * HEADS + h, first : first + count] for h in range(HEADS)], axis=1)
            dc = d_v[pl.ds(i * HEADS, HEADS), :, first : first + values].reshape(HEADS * TOK, values)
            kg = lax.dot_general(ds, qc, NT, preferred_element_type=F32) * SCALE
            vg = jnp.dot(pb, dc, preferred_element_type=F32)
            acc[: 2 * TOK, first : first + values] += kg[:, :values] + vg
            if values < count:
                acc[: 2 * TOK, first + values : first + count] += kg[:, values:]
            return carry

        lax.fori_loop(0, steps, step, 0)

    def raw_copy(half, d):
        return remote(
            parts.at[pl.ds(1, 2), halves[half]], raw.at[half, d - 1], raw_s.at[half, d - 1], raw_r.at[half, d - 1],
            across(half, d),
        )

    for e in (2, 3):
        parts[e - 1] = acc[e * TOK : (e + 1) * TOK].T.astype(BF16)
    for d in (1, 3, 2):
        for half in (0, 1):
            start(raw_copy(half, d))

    def near_copy(ch):
        rows = pl.ds(*chunks[ch])
        return remote(parts.at[0, rows], near.at[rows], near_s.at[ch], near_r.at[ch], before)

    for ch in (0, 1):
        first, count = chunks[ch]
        window_grads(first, count)
        parts[0, first : first + count] = acc[TOK : 2 * TOK, first : first + count].T.astype(BF16)
        start(near_copy(ch))

    x_own.wait()
    for d in range(SIDE):
        if d > 0:
            x_copy(d).wait_recv()
        xt[:, d * TOK : (d + 1) * TOK] = xa[d].T
    lat_ref[...] = acc[:TOK].T

    def mid_copy(half, d):
        return remote(
            mid.at[half, d - 1], back.at[half, d - 1], mid_s.at[half, d - 1], mid_r.at[half, d - 1],
            along(half, d),
        )

    for half in (0, 1):
        found = []
        for d in range(SIDE):
            src = ctx_at(x, y - d) if half == 0 else ctx_at(x - d, y)
            if d > 0:
                raw_copy(half, d).wait_recv()
            for e in range(2):
                part = parts[1 + e, halves[half]] if d == 0 else raw[half, d - 1, e]
                found.append((lst[2 + e, src], part.astype(F32)))
        for d in (1, 3, 2, 0):
            target = ctx_at(x + d, y) if half == 0 else ctx_at(x, y + d)
            added = None
            for entry, part in found:
                term = part * jnp.where(entry == target, 1.0, 0.0)
                added = term if added is None else added + term
            if d == 0:
                lat_ref[halves[half]] += added
            else:
                mid[half, d - 1] = added.astype(BF16)
                start(mid_copy(half, d))

    for ch in (0, 1):
        near_copy(ch).wait_recv()
    has_next = jnp.where(me < 15, 1.0, 0.0)
    for half in (0, 1):
        rows = halves[half]
        result = lat_ref[rows] + near[rows].astype(F32) * has_next
        for d in (1, 2, 3):
            mid_copy(half, d).wait_recv()
            result += back[half, d - 1].astype(F32)
        lat_ref[rows] = result
        gbuf[0, rows] = result.astype(BF16)

    spans = SPANS

    def g_copy(ch, d):
        rows = pl.ds(*spans[ch])
        return remote(gbuf.at[0, rows], gbuf.at[d, rows], g_s.at[ch, d - 1], g_r.at[ch, d - 1], along(0, d))

    def c_copy(ch):
        return remote(cs[ch], cr[ch], c_s.at[ch], c_r.at[ch], twin)

    def y_copy(ch, d):
        return remote(ys[ch].at[(y + d) % SIDE], yr[ch].at[d - 1], y_s.at[ch, d - 1], y_r.at[ch, d - 1], along(1, d))

    def z_copy(ch, d, owner):
        piece = zr[ch].at[owner]
        return remote(piece, piece, z_s.at[ch, d - 1], z_r.at[ch, d - 1], {"dp": (dp + 2 * d) % n_dp})

    def f_copy(ch, owner):
        piece = fin[ch].at[owner]
        return remote(piece, piece, f_s.at[ch], f_r.at[ch], twin)

    n_z = n_dp // 2
    part = fin[0].shape[1]

    def slot(ch, row, half):
        at, wide = divmod(ch, 2)
        return dp_v.at[at * 2 * SIDE + row * 2 + half, pl.ds(0, part), pl.ds(256 * wide, cs[ch].shape[2])]

    def multiply(ch):
        for d in (1, 2, 3):
            g_copy(ch, d).wait_recv()
        gt = jnp.concatenate([gbuf[d, pl.ds(*spans[ch])] for d in range(SIDE)], axis=1)
        spare = cs[ch].shape[2] - gt.shape[0]
        if spare:
            gt = jnp.concatenate([gt, jnp.zeros((spare, gt.shape[1]), BF16)], axis=0)
        weight = lax.dot_general(xt[...], gt, NT, preferred_element_type=F32)
        for i in range(2 * SIDE):
            slot(ch, i // 2, i % 2)[...] = weight[i * part : (i + 1) * part]
        for i in range(SIDE):
            cs[ch][i] = slot(ch, i, 1 - core)[...].astype(BF16)
        start(c_copy(ch))

    def add_core(ch):
        c_copy(ch).wait_recv()
        for i in range(SIDE):
            both = slot(ch, i, core)[...] + cr[ch][i].astype(F32)
            slot(ch, i, core)[...] = both
            ys[ch][i] = both.astype(BF16)
        for d in (1, 3, 2):
            start(y_copy(ch, d))

    def add_y(ch):
        added = slot(ch, y, core)[...]
        for d in (1, 2, 3):
            y_copy(ch, d).wait_recv()
            added += yr[ch][d - 1].astype(F32)
        zr[ch][z] = added.astype(BF16)
        for d in range(1, n_z):
            start(z_copy(ch, d, z))

    def add_z(ch):
        for d in range(1, n_z):
            z_copy(ch, d, (z + n_z - d) % n_z).wait_recv()
        added = zr[ch][0].astype(F32)
        for i in range(1, n_z):
            added += zr[ch][i].astype(F32)
        fin[ch][core] = added
        start(f_copy(ch, core))

    def put(ch):
        f_copy(ch, 1 - core).wait_recv()
        first, count = spans[ch]
        for i in (0, 1):
            w_ref[i * part : (i + 1) * part, first : first + count] = fin[ch][i, :, :count]

    for ch in range(len(spans)):
        for d in (1, 3, 2):
            start(g_copy(ch, d))
    stages = ((0, multiply), (0, add_core), (1, add_y), (2, add_z), (3, put))
    for turn in range(len(spans) + 3):
        for late, stage_of in stages:
            if 0 <= turn - late < len(spans):
                stage_of(turn - late)
    for c in started:
        c.wait_send()

    @pl.when(y == SIDE - 1)
    def _():
        prev_copy(1).wait_send()


def per_device(queries, latents, out_grad, layer_input, block_list):
    n_dp = lax.axis_size("dp")
    n_z = n_dp // 2
    n_heads = queries.shape[2]
    cols = layer_input.shape[2] // 16
    vmem = pl.BlockSpec(memory_space=pltpu.VMEM)
    hbm = pl.BlockSpec(memory_space=pl.ANY)
    dma = pltpu.SemaphoreType.DMA
    v = pltpu.VMEM
    widths = [(count + 127) // 128 * 128 for _, count in SPANS]
    n = len(SPANS)
    part = cols // 2
    lat_t, weight_grad = pl.pallas_call(
        kernel,
        out_shape=[jax.ShapeDtypeStruct((W, TOK), F32), jax.ShapeDtypeStruct((cols, W), F32)],
        in_specs=[pl.BlockSpec(memory_space=pltpu.SMEM), hbm, hbm, hbm, hbm],
        out_specs=[vmem, vmem],
        scratch_shapes=[
            v((n_heads, W, TOK), BF16),
            v((2, TOK, HEADS, R), BF16),
            v((n_heads, TOK, R), BF16),
            v((2, SIDE, HALF, TOK), BF16),
            v((2, 3, 2, HALF, TOK), BF16),
            v((2, SIDE, 2, HALF, TOK), BF16),
            v((2, HALF, TOK), BF16),
            v((SLOTS * TOK, W), BF16),
            v((n_heads // SUB, 2 * TOK, SUB * TOK), F32),
            v((n_heads // SUB, 2 * TOK, SUB * TOK), F32),
            v((SLOTS * TOK, W), F32),
            v((3, W, TOK), BF16),
            v((2, 3, 2, HALF, TOK), BF16),
            v((2, 3, HALF, TOK), BF16),
            v((2, 3, HALF, TOK), BF16),
            v((W, TOK), BF16),
            v((SIDE, W, TOK), BF16),
            v((SIDE, TOK, SIDE * cols), BF16),
            v((SIDE * cols, SIDE * TOK), BF16),
            [v((SIDE, part, w), BF16) for w in widths],
            [v((SIDE, part, w), BF16) for w in widths],
            [v((SIDE, part, w), BF16) for w in widths],
            [v((3, part, w), BF16) for w in widths],
            [v((n_z, part, w), BF16) for w in widths],
            [v((2, part, w), F32) for w in widths],
            dma((n_heads // HEADS,)), dma((2,)), dma((2,)), dma((2, 3)), dma((2, 3)), dma((2, 3)), dma((2, 3)), dma((2,)), dma((2,)),
            dma((3,)), dma((3,)), dma, dma((2, 3)), dma((2, 3)), dma((2, 3)), dma((2, 3)), dma((2,)), dma((2,)),
            dma((n, 3)), dma((n, 3)), dma((n,)), dma((n,)), dma((n, 3)), dma((n, 3)),
            dma((n, n_z - 1)), dma((n, n_z - 1)), dma((n,)), dma((n,)),
        ],
        compiler_params=pltpu.CompilerParams(
            collective_id=0, has_side_effects=True, vmem_limit_bytes=60 * 2**20
        ),
        name="attention_backward",
    )(
        block_list[0].T,
        latents.transpose(0, 2, 1),
        queries[0].transpose(1, 2, 0),
        out_grad[0],
        layer_input[0],
    )
    return (lat_t.T[None], weight_grad)


def solution(mesh):
    placed = (
        P("dp", "ctx", None, None),
        P("dp", "ctx", None),
        P("dp", "ctx", None, None),
        P("dp", "ctx", None),
        P("dp", None, None),
    )
    return jax.shard_map(
        per_device,
        mesh=mesh,
        in_specs=placed,
        out_specs=(P("dp", "ctx", None), P("ctx", None)),
        check_vma=False,
    )
```

```python
import jax
import jax.numpy as jnp
from jax import lax
from jax.experimental import pallas as pl
from jax.experimental.pallas import tpu as pltpu
from jax.sharding import PartitionSpec as P

R = 512
W = 576
HALF = 288
TOK = 128
SLOTS = 4
SIDE = 4
HEADS = 16
SUB = 4
SPANS = ((0, 128), (128, 192), (320, 128), (448, 128))
SCALE = 192 ** -0.5
LOG2E = 1.4426950408889634
NT = (((1,), (1,)), ((), ()))
MESH = pl.DeviceIdType.MESH
F32 = jnp.float32
BF16 = jnp.bfloat16
TOP, LOW = pl.ds(0, HALF), pl.ds(HALF, HALF)


def place():
    me = lax.axis_index("ctx")
    return me, me // SIDE, me % SIDE


def ctx_at(x, y):
    return (x % SIDE) * SIDE + y % SIDE


def remote(src, dst, send, recv, device):
    return pltpu.make_async_remote_copy(
        src_ref=src, dst_ref=dst, send_sem=send, recv_sem=recv, device_id=device, device_id_type=MESH
    )


def greet(devices):
    barrier = pltpu.get_barrier_semaphore()
    for device in devices:
        pl.semaphore_signal(barrier, inc=1, device_id=device, device_id_type=MESH)
    pl.semaphore_wait(barrier, len(devices))


def line_peers(x, y):
    return [{"ctx": ctx_at(x + d, y)} for d in (1, 2, 3)] + [{"ctx": ctx_at(x, y + d)} for d in (1, 2, 3)]


def kernel(
    lst, lat, qt, do, inp, lat_ref, w_ref,
    q_v, stage, d_v, line, sel, got, prev, k_v, s_v, dp_v, acc, parts, raw, mid, back, near, gbuf, xa, xt,
    cs, cr, ys, yr, zr, fin,
    q_s, do_s, own_s, line_s, line_r, sel_s, sel_r, prev_s, prev_r, x_s, x_r, xo_s, raw_s, raw_r, mid_s, mid_r, near_s, near_r,
    g_s, g_r, c_s, c_r, y_s, y_r, z_s, z_r, f_s, f_r,
):
    me, x, y = place()
    dp = lax.axis_index("dp")
    n_dp = lax.axis_size("dp")
    core, z = dp % 2, dp // 2
    twin = {"dp": dp + 1 - 2 * core}
    after, before = {"ctx": (me + 1) % 16}, {"ctx": (me + 15) % 16}
    n_heads = q_v.shape[0]
    steps = n_heads // HEADS
    quarter = xa.shape[2]
    started = []

    def start(c):
        c.start()
        started.append(c)

    def do_load(i):
        return pltpu.make_async_copy(do.at[:, pl.ds(i * HEADS, HEADS)], stage.at[i % 2], do_s.at[i % 2])

    def q_load(i):
        part = pl.ds(i * HEADS, HEADS)
        return pltpu.make_async_copy(qt.at[part], q_v.at[part], q_s.at[i])

    halves = (TOP, LOW)
    chunks = ((0, 256), (256, W - 256))
    mine = (line.at[0, x], line.at[1, y])
    own_loads = [pltpu.make_async_copy(lat.at[0, halves[h]], mine[h], own_s.at[h]) for h in (0, 1)]
    for load in own_loads:
        load.start()
    do_load(0).start()
    q_load(0).start()
    x_own = pltpu.make_async_copy(
        inp.at[:, pl.ds(pl.multiple_of(x * quarter, 128), quarter)], xa.at[0], xo_s
    )
    greet(
        line_peers(x, y) + [after, before, twin] + [{"dp": (dp + 2 * d) % n_dp} for d in range(1, n_dp // 2)]
    )
    for load in own_loads:
        load.wait()

    def along(half, d):
        return {"ctx": ctx_at(x + d, y) if half == 0 else ctx_at(x, y + d)}

    def across(half, d):
        return along(1 - half, d)

    def line_copy(half, d):
        return remote(mine[half], mine[half], line_s.at[half, d - 1], line_r.at[half, d - 1], along(half, d))

    def line_wait(half, d):
        slot = line.at[0, (x + SIDE - d) % SIDE] if half == 0 else line.at[1, (y + SIDE - d) % SIDE]
        remote(slot, slot, line_s.at[half, d - 1], line_r.at[half, d - 1], along(half, d)).wait_recv()

    def prev_copy(half):
        return remote(mine[half], prev.at[half], prev_s.at[half], prev_r.at[half], after)

    for d in (1, 3, 2):
        for half in (0, 1):
            start(line_copy(half, d))
    start(prev_copy(0))

    @pl.when(y == SIDE - 1)
    def _():
        prev_copy(1).start()

    do_load(1).start()
    q_load(1).start()
    x_own.start()

    k_v[:TOK] = jnp.concatenate([line[0, x], line[1, y]], axis=0).T
    def listed(device, e):
        block = jnp.maximum(lst[2 + e, device], 0)
        return block >> 2, block & 3

    def sel_copy(half, d):
        return remote(
            sel.at[half, d - 1], got.at[half, d], sel_s.at[half, d - 1], sel_r.at[half, d - 1], across(half, d)
        )

    def pass_on():
        for half in (0, 1):
            for d in (1, 2, 3):
                line_wait(half, d)
        for d in (1, 3, 2, 0):
            for half in (0, 1):
                for e in (0, 1):
                    wanted = listed(across(half, d)["ctx"], e)[half]
                    if d == 0:
                        got[half, 0, e] = line[half, wanted]
                    else:
                        sel[half, d - 1, e] = line[half, wanted]
                if d > 0:
                    start(sel_copy(half, d))

    def columns(at):
        return (
            jnp.concatenate([q_v[at * SUB + i] for i in range(SUB)], axis=1),
            d_v[pl.ds(at * SUB, SUB)].reshape(SUB * TOK, R),
        )

    def products(keys, qc, dc):
        return (
            jnp.dot(keys, qc, preferred_element_type=F32),
            lax.dot_general(keys[:, :R], dc, NT, preferred_element_type=F32),
        )

    per = HEADS // SUB

    def arrange(i):
        do_load(i).wait()
        q_load(i).wait()
        d_v[i * HEADS : (i + 1) * HEADS] = jnp.swapaxes(stage[i % 2], 0, 1)
        if i + 2 < steps:
            do_load(i + 2).start()
            q_load(i + 2).start()

    def window_products(i, rows):
        keys = k_v[rows]
        for k in range(per):
            at = i * per + k
            s_v[at, rows], dp_v[at, rows] = products(keys, *columns(at))

    for i in range(steps // 2):
        arrange(i)
        window_products(i, pl.ds(0, TOK))
        if i == 0:
            pass_on()
    prev_copy(0).wait_recv()

    @pl.when(y == 0)
    def _():
        prev_copy(1).wait_recv()
        k_v[TOK : 2 * TOK] = jnp.concatenate([prev[0], prev[1]], axis=0).T

    @pl.when(y > 0)
    def _():
        k_v[TOK : 2 * TOK] = jnp.concatenate([prev[0], line[1, (y + SIDE - 1) % SIDE]], axis=0).T

    for i in range(steps // 2, steps):
        arrange(i)
        window_products(i, pl.ds(0, 2 * TOK))
    for i in range(steps // 2):
        window_products(i, pl.ds(TOK, TOK))
    for half in (0, 1):
        for d in (1, 2, 3):
            sel_copy(half, d).wait_recv()

    def x_copy(d):
        to = (x + d) % SIDE
        return remote(
            inp.at[:, pl.ds(pl.multiple_of(to * quarter, 128), quarter)],
            xa.at[d], x_s.at[d - 1], x_r.at[d - 1], {"ctx": ctx_at(x + d, y)},
        )

    for d in (1, 3, 2):
        start(x_copy(d))

    for e in (0, 1):
        bx, by = listed(me, e)
        k_v[(2 + e) * TOK : (3 + e) * TOK] = jnp.concatenate(
            [got[0, (y - by) & 3, e], got[1, (x - bx) & 3, e]], axis=0
        ).T
    acc[...] = jnp.zeros_like(acc)
    key_at = lax.broadcasted_iota(jnp.int32, (TOK, TOK), 0)
    tok_at = lax.broadcasted_iota(jnp.int32, (TOK, TOK), 1)
    causal = jnp.concatenate([key_at <= tok_at] * SUB, axis=1)
    away = [None] + [jnp.where(lst[e, me] >= 0, 0.0, jnp.inf) for e in range(1, SLOTS)]
    c = SCALE * LOG2E

    def softmax(at):
        qc, dc = columns(at)
        s_far, dp_far = products(k_v[2 * TOK :], qc, dc)
        ss = [s_v[at, :TOK], s_v[at, TOK:], s_far[:TOK], s_far[TOK:]]
        dprob = jnp.concatenate([dp_v[at], dp_far], axis=0)
        ss[0] = jnp.where(causal, ss[0], -jnp.inf)
        top = jnp.max(ss[0], axis=0, keepdims=True)
        for e in range(1, SLOTS):
            top = jnp.maximum(top, jnp.max(ss[e], axis=0, keepdims=True) - away[e])
        mc = top * c
        p = jnp.concatenate(
            [jnp.exp2(ss[e] * c - (mc if e == 0 else mc + away[e])) for e in range(SLOTS)], axis=0
        )
        inv = 1.0 / jnp.sum(p, axis=0, keepdims=True)
        delta = jnp.sum(p * dprob, axis=0, keepdims=True) * inv
        probs = p * inv
        dscore = probs * (dprob - delta)
        s_v[at] = probs[: 2 * TOK]
        dp_v[at] = dscore[: 2 * TOK]
        return qc, dc, probs[2 * TOK :].astype(BF16), dscore[2 * TOK :].astype(BF16)

    def grads(qc, dc, pb, ds):
        kg = lax.dot_general(ds, qc, NT, preferred_element_type=F32) * SCALE
        vg = jnp.dot(pb, dc, preferred_element_type=F32)
        acc[2 * TOK :, :R] += kg[:, :R] + vg
        acc[2 * TOK :, R:] += kg[:, R:]

    def attend(i, carry):
        held = None
        for k in range(per):
            fresh = softmax(i * per + k)
            if held is not None:
                grads(*held)
            held = fresh
        grads(*held)
        return carry

    lax.fori_loop(0, steps, attend, 0)

    def window_grads(first, count):
        values = min(count, R - first)

        def step(i, carry):
            ats = [i * per + k for k in range(per)]
            ds = jnp.concatenate([dp_v[at].astype(BF16) for at in ats], axis=1)
            pb = jnp.concatenate([s_v[at].astype(BF16) for at in ats], axis=1)
            qc = jnp.concatenate([q_v[i * HEADS + h, first : first + count] for h in range(HEADS)], axis=1)
            dc = d_v[pl.ds(i * HEADS, HEADS), :, first : first + values].reshape(HEADS * TOK, values)
            kg = lax.dot_general(ds, qc, NT, preferred_element_type=F32) * SCALE
            vg = jnp.dot(pb, dc, preferred_element_type=F32)
            acc[: 2 * TOK, first : first + values] += kg[:, :values] + vg
            if values < count:
                acc[: 2 * TOK, first + values : first + count] += kg[:, values:]
            return carry

        lax.fori_loop(0, steps, step, 0)

    def raw_copy(half, d):
        return remote(
            parts.at[pl.ds(1, 2), halves[half]], raw.at[half, d - 1], raw_s.at[half, d - 1], raw_r.at[half, d - 1],
            across(half, d),
        )

    for e in (2, 3):
        parts[e - 1] = acc[e * TOK : (e + 1) * TOK].T.astype(BF16)
    for d in (1, 3, 2):
        for half in (0, 1):
            start(raw_copy(half, d))

    def near_copy(half):
        return remote(parts.at[0, halves[half]], near.at[half], near_s.at[half], near_r.at[half], before)

    for first, count in chunks:
        window_grads(first, count)
    parts[0] = acc[TOK : 2 * TOK].T.astype(BF16)
    start(near_copy(0))

    @pl.when(y == 0)
    def _():
        near_copy(1).start()

    x_own.wait()
    for d in range(SIDE):
        if d > 0:
            x_copy(d).wait_recv()
        xt[:, d * TOK : (d + 1) * TOK] = xa[d].T
    lat_ref[...] = acc[:TOK].T

    def mid_copy(half, d):
        return remote(
            mid.at[half, d - 1], back.at[half, d - 1], mid_s.at[half, d - 1], mid_r.at[half, d - 1],
            along(half, d),
        )

    for half in (0, 1):
        found = []
        for d in range(SIDE):
            src = ctx_at(x, y - d) if half == 0 else ctx_at(x - d, y)
            if d > 0:
                raw_copy(half, d).wait_recv()
            for e in range(2):
                part = parts[1 + e, halves[half]] if d == 0 else raw[half, d - 1, e]
                found.append((lst[2 + e, src], part.astype(F32)))
        for d in (1, 3, 2, 0):
            target = ctx_at(x + d, y) if half == 0 else ctx_at(x, y + d)
            added = None
            for entry, part in found:
                term = part * jnp.where(entry == target, 1.0, 0.0)
                added = term if added is None else added + term
            if half == 1 and d == 3:
                added += parts[0, halves[1]].astype(F32) * jnp.where(y > 0, 1.0, 0.0)
            if d == 0:
                lat_ref[halves[half]] += added
            else:
                mid[half, d - 1] = added.astype(BF16)
                start(mid_copy(half, d))

    near_copy(0).wait_recv()
    has_next = jnp.where(me < 15, 1.0, 0.0)

    @pl.when(y == SIDE - 1)
    def _():
        near_copy(1).wait_recv()
        lat_ref[LOW] += near[1].astype(F32) * has_next

    lat_ref[TOP] += near[0].astype(F32) * has_next
    for half in (0, 1):
        rows = halves[half]
        result = lat_ref[rows]
        for d in (1, 2, 3):
            mid_copy(half, d).wait_recv()
            result += back[half, d - 1].astype(F32)
        lat_ref[rows] = result
        gbuf[0, rows] = result.astype(BF16)

    spans = SPANS

    def g_copy(ch, d):
        rows = pl.ds(*spans[ch])
        return remote(gbuf.at[0, rows], gbuf.at[d, rows], g_s.at[ch, d - 1], g_r.at[ch, d - 1], along(0, d))

    def c_copy(ch):
        return remote(cs[ch], cr[ch], c_s.at[ch], c_r.at[ch], twin)

    def y_copy(ch, d):
        return remote(ys[ch].at[(y + d) % SIDE], yr[ch].at[d - 1], y_s.at[ch, d - 1], y_r.at[ch, d - 1], along(1, d))

    def z_copy(ch, d, owner):
        piece = zr[ch].at[owner]
        return remote(piece, piece, z_s.at[ch, d - 1], z_r.at[ch, d - 1], {"dp": (dp + 2 * d) % n_dp})

    def f_copy(ch, owner):
        piece = fin[ch].at[owner]
        return remote(piece, piece, f_s.at[ch], f_r.at[ch], twin)

    n_z = n_dp // 2
    part = fin[0].shape[1]

    def slot(ch, row, half):
        at, wide = divmod(ch, 2)
        return dp_v.at[at * 2 * SIDE + row * 2 + half, pl.ds(0, part), pl.ds(256 * wide, cs[ch].shape[2])]

    def multiply(ch):
        for d in (1, 2, 3):
            g_copy(ch, d).wait_recv()
        gt = jnp.concatenate([gbuf[d, pl.ds(*spans[ch])] for d in range(SIDE)], axis=1)
        spare = cs[ch].shape[2] - gt.shape[0]
        if spare:
            gt = jnp.concatenate([gt, jnp.zeros((spare, gt.shape[1]), BF16)], axis=0)
        weight = lax.dot_general(xt[...], gt, NT, preferred_element_type=F32)
        for i in range(2 * SIDE):
            slot(ch, i // 2, i % 2)[...] = weight[i * part : (i + 1) * part]
        for i in range(SIDE):
            cs[ch][i] = slot(ch, i, 1 - core)[...].astype(BF16)
        start(c_copy(ch))

    def add_core(ch):
        c_copy(ch).wait_recv()
        for i in range(SIDE):
            both = slot(ch, i, core)[...] + cr[ch][i].astype(F32)
            slot(ch, i, core)[...] = both
            ys[ch][i] = both.astype(BF16)
        for d in (1, 3, 2):
            start(y_copy(ch, d))

    def add_y(ch):
        added = slot(ch, y, core)[...]
        for d in (1, 2, 3):
            y_copy(ch, d).wait_recv()
            added += yr[ch][d - 1].astype(F32)
        zr[ch][z] = added.astype(BF16)
        for d in range(1, n_z):
            start(z_copy(ch, d, z))

    def add_z(ch):
        for d in range(1, n_z):
            z_copy(ch, d, (z + n_z - d) % n_z).wait_recv()
        added = zr[ch][0].astype(F32)
        for i in range(1, n_z):
            added += zr[ch][i].astype(F32)
        fin[ch][core] = added
        start(f_copy(ch, core))

    def put(ch):
        f_copy(ch, 1 - core).wait_recv()
        first, count = spans[ch]
        for i in (0, 1):
            w_ref[i * part : (i + 1) * part, first : first + count] = fin[ch][i, :, :count]

    for ch in range(len(spans)):
        for d in (1, 3, 2):
            start(g_copy(ch, d))
    stages = ((0, multiply), (1, add_core), (2, add_y), (3, add_z), (4, put))
    for turn in range(len(spans) + 4):
        for late, stage_of in stages:
            if 0 <= turn - late < len(spans):
                stage_of(turn - late)
    for c in started:
        c.wait_send()

    @pl.when(y == SIDE - 1)
    def _():
        prev_copy(1).wait_send()

    @pl.when(y == 0)
    def _():
        near_copy(1).wait_send()


def per_device(queries, latents, out_grad, layer_input, block_list):
    n_dp = lax.axis_size("dp")
    n_z = n_dp // 2
    n_heads = queries.shape[2]
    cols = layer_input.shape[2] // 16
    vmem = pl.BlockSpec(memory_space=pltpu.VMEM)
    hbm = pl.BlockSpec(memory_space=pl.ANY)
    dma = pltpu.SemaphoreType.DMA
    v = pltpu.VMEM
    widths = [(count + 127) // 128 * 128 for _, count in SPANS]
    n = len(SPANS)
    part = cols // 2
    lat_t, weight_grad = pl.pallas_call(
        kernel,
        out_shape=[jax.ShapeDtypeStruct((W, TOK), F32), jax.ShapeDtypeStruct((cols, W), F32)],
        in_specs=[pl.BlockSpec(memory_space=pltpu.SMEM), hbm, hbm, hbm, hbm],
        out_specs=[vmem, vmem],
        scratch_shapes=[
            v((n_heads, W, TOK), BF16),
            v((2, TOK, HEADS, R), BF16),
            v((n_heads, TOK, R), BF16),
            v((2, SIDE, HALF, TOK), BF16),
            v((2, 3, 2, HALF, TOK), BF16),
            v((2, SIDE, 2, HALF, TOK), BF16),
            v((2, HALF, TOK), BF16),
            v((SLOTS * TOK, W), BF16),
            v((n_heads // SUB, 2 * TOK, SUB * TOK), F32),
            v((n_heads // SUB, 2 * TOK, SUB * TOK), F32),
            v((SLOTS * TOK, W), F32),
            v((3, W, TOK), BF16),
            v((2, 3, 2, HALF, TOK), BF16),
            v((2, 3, HALF, TOK), BF16),
            v((2, 3, HALF, TOK), BF16),
            v((2, HALF, TOK), BF16),
            v((SIDE, W, TOK), BF16),
            v((SIDE, TOK, SIDE * cols), BF16),
            v((SIDE * cols, SIDE * TOK), BF16),
            [v((SIDE, part, w), BF16) for w in widths],
            [v((SIDE, part, w), BF16) for w in widths],
            [v((SIDE, part, w), BF16) for w in widths],
            [v((3, part, w), BF16) for w in widths],
            [v((n_z, part, w), BF16) for w in widths],
            [v((2, part, w), F32) for w in widths],
            dma((n_heads // HEADS,)), dma((2,)), dma((2,)), dma((2, 3)), dma((2, 3)), dma((2, 3)), dma((2, 3)), dma((2,)), dma((2,)),
            dma((3,)), dma((3,)), dma, dma((2, 3)), dma((2, 3)), dma((2, 3)), dma((2, 3)), dma((2,)), dma((2,)),
            dma((n, 3)), dma((n, 3)), dma((n,)), dma((n,)), dma((n, 3)), dma((n, 3)),
            dma((n, n_z - 1)), dma((n, n_z - 1)), dma((n,)), dma((n,)),
        ],
        compiler_params=pltpu.CompilerParams(
            collective_id=0, has_side_effects=True, vmem_limit_bytes=60 * 2**20
        ),
        name="attention_backward",
    )(
        block_list[0].T,
        latents.transpose(0, 2, 1),
        queries[0].transpose(1, 2, 0),
        out_grad[0],
        layer_input[0],
    )
    return (lat_t.T[None], weight_grad)


def solution(mesh):
    placed = (
        P("dp", "ctx", None, None),
        P("dp", "ctx", None),
        P("dp", "ctx", None, None),
        P("dp", "ctx", None),
        P("dp", None, None),
    )
    return jax.shard_map(
        per_device,
        mesh=mesh,
        in_specs=placed,
        out_specs=(P("dp", "ctx", None), P("ctx", None)),
        check_vma=False,
    )
```

```python
import jax
import jax.numpy as jnp
from jax import lax
from jax.experimental import pallas as pl
from jax.experimental.pallas import tpu as pltpu
from jax.sharding import PartitionSpec as P

R = 512
W = 576
HALF = 288
TOK = 128
SLOTS = 4
SIDE = 4
HEADS = 16
SUB = 4
SPANS = ((0, 256), (256, 192), (448, 128))
SCALE = 192 ** -0.5
LOG2E = 1.4426950408889634
NT = (((1,), (1,)), ((), ()))
MESH = pl.DeviceIdType.MESH
F32 = jnp.float32
BF16 = jnp.bfloat16
TOP, LOW = pl.ds(0, HALF), pl.ds(HALF, HALF)


def place():
    me = lax.axis_index("ctx")
    return me, me // SIDE, me % SIDE


def ctx_at(x, y):
    return (x % SIDE) * SIDE + y % SIDE


def remote(src, dst, send, recv, device):
    return pltpu.make_async_remote_copy(
        src_ref=src, dst_ref=dst, send_sem=send, recv_sem=recv, device_id=device, device_id_type=MESH
    )


def greet(devices):
    barrier = pltpu.get_barrier_semaphore()
    for device in devices:
        pl.semaphore_signal(barrier, inc=1, device_id=device, device_id_type=MESH)
    pl.semaphore_wait(barrier, len(devices))


def line_peers(x, y):
    return [{"ctx": ctx_at(x + d, y)} for d in (1, 2, 3)] + [{"ctx": ctx_at(x, y + d)} for d in (1, 2, 3)]


def kernel(
    lst, lat, qt, do, inp, lat_ref, w_ref,
    q_v, stage, d_v, line, sel, got, prev, k_v, s_v, dp_v, acc, parts, raw, mid, back, near, gbuf, xa, xt,
    cs, cr, ys, yr, zr, fin,
    q_s, do_s, own_s, line_s, line_r, sel_s, sel_r, prev_s, prev_r, x_s, x_r, xo_s, raw_s, raw_r, mid_s, mid_r, near_s, near_r,
    g_s, g_r, c_s, c_r, y_s, y_r, z_s, z_r, f_s, f_r,
):
    me, x, y = place()
    dp = lax.axis_index("dp")
    n_dp = lax.axis_size("dp")
    core, z = dp % 2, dp // 2
    twin = {"dp": dp + 1 - 2 * core}
    after, before = {"ctx": (me + 1) % 16}, {"ctx": (me + 15) % 16}
    n_heads = q_v.shape[0]
    steps = n_heads // HEADS
    quarter = xa.shape[2]
    started = []

    def start(c):
        c.start()
        started.append(c)

    def do_load(i):
        return pltpu.make_async_copy(do.at[:, pl.ds(i * HEADS, HEADS)], stage.at[i % 2], do_s.at[i % 2])

    def q_load(i):
        part = pl.ds(i * HEADS, HEADS)
        return pltpu.make_async_copy(qt.at[part], q_v.at[part], q_s.at[i])

    halves = (TOP, LOW)
    chunks = ((0, 256), (256, W - 256))
    mine = (line.at[0, x], line.at[1, y])
    own_loads = [pltpu.make_async_copy(lat.at[0, halves[h]], mine[h], own_s.at[h]) for h in (0, 1)]
    for load in own_loads:
        load.start()
    do_load(0).start()
    q_load(0).start()
    x_own = pltpu.make_async_copy(
        inp.at[:, pl.ds(pl.multiple_of(x * quarter, 128), quarter)], xa.at[0], xo_s
    )
    greet(
        line_peers(x, y) + [after, before, twin] + [{"dp": (dp + 2 * d) % n_dp} for d in range(1, n_dp // 2)]
    )
    for load in own_loads:
        load.wait()

    def along(half, d):
        return {"ctx": ctx_at(x + d, y) if half == 0 else ctx_at(x, y + d)}

    def across(half, d):
        return along(1 - half, d)

    def line_copy(half, d):
        return remote(mine[half], mine[half], line_s.at[half, d - 1], line_r.at[half, d - 1], along(half, d))

    def line_wait(half, d):
        slot = line.at[0, (x + SIDE - d) % SIDE] if half == 0 else line.at[1, (y + SIDE - d) % SIDE]
        remote(slot, slot, line_s.at[half, d - 1], line_r.at[half, d - 1], along(half, d)).wait_recv()

    def prev_copy(half):
        return remote(mine[half], prev.at[half], prev_s.at[half], prev_r.at[half], after)

    for d in (1, 3, 2):
        for half in (0, 1):
            start(line_copy(half, d))
    start(prev_copy(0))

    @pl.when(y == SIDE - 1)
    def _():
        prev_copy(1).start()

    do_load(1).start()
    q_load(1).start()
    x_own.start()

    k_v[:TOK] = jnp.concatenate([line[0, x], line[1, y]], axis=0).T
    def listed(device, e):
        block = jnp.maximum(lst[2 + e, device], 0)
        return block >> 2, block & 3

    def sel_copy(half, d):
        return remote(
            sel.at[half, d - 1], got.at[half, d], sel_s.at[half, d - 1], sel_r.at[half, d - 1], across(half, d)
        )

    def pass_on():
        for half in (0, 1):
            for d in (1, 2, 3):
                line_wait(half, d)
        for d in (1, 3, 2, 0):
            for half in (0, 1):
                for e in (0, 1):
                    wanted = listed(across(half, d)["ctx"], e)[half]
                    if d == 0:
                        got[half, 0, e] = line[half, wanted]
                    else:
                        sel[half, d - 1, e] = line[half, wanted]
                if d > 0:
                    start(sel_copy(half, d))

    def columns(at):
        return (
            jnp.concatenate([q_v[at * SUB + i] for i in range(SUB)], axis=1),
            d_v[pl.ds(at * SUB, SUB)].reshape(SUB * TOK, R),
        )

    def products(keys, qc, dc):
        return (
            jnp.dot(keys, qc, preferred_element_type=F32),
            lax.dot_general(keys[:, :R], dc, NT, preferred_element_type=F32),
        )

    per = HEADS // SUB

    def arrange(i):
        do_load(i).wait()
        q_load(i).wait()
        d_v[i * HEADS : (i + 1) * HEADS] = jnp.swapaxes(stage[i % 2], 0, 1)
        if i + 2 < steps:
            do_load(i + 2).start()
            q_load(i + 2).start()

    def window_products(i, rows):
        keys = k_v[rows]
        for k in range(per):
            at = i * per + k
            s_v[at, rows], dp_v[at, rows] = products(keys, *columns(at))

    for i in range(steps // 2):
        arrange(i)
        window_products(i, pl.ds(0, TOK))
        if i == 0:
            pass_on()
    prev_copy(0).wait_recv()

    @pl.when(y == 0)
    def _():
        prev_copy(1).wait_recv()
        k_v[TOK : 2 * TOK] = jnp.concatenate([prev[0], prev[1]], axis=0).T

    @pl.when(y > 0)
    def _():
        k_v[TOK : 2 * TOK] = jnp.concatenate([prev[0], line[1, (y + SIDE - 1) % SIDE]], axis=0).T

    for i in range(steps // 2, steps):
        arrange(i)
        window_products(i, pl.ds(0, 2 * TOK))
    for i in range(steps // 2):
        window_products(i, pl.ds(TOK, TOK))
    for half in (0, 1):
        for d in (1, 2, 3):
            sel_copy(half, d).wait_recv()

    def x_copy(d):
        to = (x + d) % SIDE
        return remote(
            inp.at[:, pl.ds(pl.multiple_of(to * quarter, 128), quarter)],
            xa.at[d], x_s.at[d - 1], x_r.at[d - 1], {"ctx": ctx_at(x + d, y)},
        )

    for d in (1, 3, 2):
        start(x_copy(d))

    for e in (0, 1):
        bx, by = listed(me, e)
        k_v[(2 + e) * TOK : (3 + e) * TOK] = jnp.concatenate(
            [got[0, (y - by) & 3, e], got[1, (x - bx) & 3, e]], axis=0
        ).T
    acc[...] = jnp.zeros_like(acc)
    key_at = lax.broadcasted_iota(jnp.int32, (TOK, TOK), 0)
    tok_at = lax.broadcasted_iota(jnp.int32, (TOK, TOK), 1)
    causal = jnp.concatenate([key_at <= tok_at] * SUB, axis=1)
    away = [None] + [jnp.where(lst[e, me] >= 0, 0.0, jnp.inf) for e in range(1, SLOTS)]
    c = SCALE * LOG2E

    def softmax(at):
        qc, dc = columns(at)
        s_far, dp_far = products(k_v[2 * TOK :], qc, dc)
        ss = [s_v[at, :TOK], s_v[at, TOK:], s_far[:TOK], s_far[TOK:]]
        dprob = jnp.concatenate([dp_v[at], dp_far], axis=0)
        ss[0] = jnp.where(causal, ss[0], -jnp.inf)
        top = jnp.max(ss[0], axis=0, keepdims=True)
        for e in range(1, SLOTS):
            top = jnp.maximum(top, jnp.max(ss[e], axis=0, keepdims=True) - away[e])
        mc = top * c
        p = jnp.concatenate(
            [jnp.exp2(ss[e] * c - (mc if e == 0 else mc + away[e])) for e in range(SLOTS)], axis=0
        )
        inv = 1.0 / jnp.sum(p, axis=0, keepdims=True)
        delta = jnp.sum(p * dprob, axis=0, keepdims=True) * inv
        probs = p * inv
        dscore = probs * (dprob - delta)
        s_v[at] = probs[: 2 * TOK]
        dp_v[at] = dscore[: 2 * TOK]
        return qc, dc, probs[2 * TOK :].astype(BF16), dscore[2 * TOK :].astype(BF16)

    def grads(qc, dc, pb, ds):
        kg = lax.dot_general(ds, qc, NT, preferred_element_type=F32) * SCALE
        vg = jnp.dot(pb, dc, preferred_element_type=F32)
        acc[2 * TOK :, :R] += kg[:, :R] + vg
        acc[2 * TOK :, R:] += kg[:, R:]

    def attend(i, carry):
        held = None
        for k in range(per):
            fresh = softmax(i * per + k)
            if held is not None:
                grads(*held)
            held = fresh
        grads(*held)
        return carry

    lax.fori_loop(0, steps, attend, 0)

    def window_grads(first, count):
        values = min(count, R - first)

        def step(i, carry):
            ats = [i * per + k for k in range(per)]
            ds = jnp.concatenate([dp_v[at].astype(BF16) for at in ats], axis=1)
            pb = jnp.concatenate([s_v[at].astype(BF16) for at in ats], axis=1)
            qc = jnp.concatenate([q_v[i * HEADS + h, first : first + count] for h in range(HEADS)], axis=1)
            dc = d_v[pl.ds(i * HEADS, HEADS), :, first : first + values].reshape(HEADS * TOK, values)
            kg = lax.dot_general(ds, qc, NT, preferred_element_type=F32) * SCALE
            vg = jnp.dot(pb, dc, preferred_element_type=F32)
            acc[: 2 * TOK, first : first + values] += kg[:, :values] + vg
            if values < count:
                acc[: 2 * TOK, first + values : first + count] += kg[:, values:]
            return carry

        lax.fori_loop(0, steps, step, 0)

    def raw_copy(half, d):
        return remote(
            parts.at[pl.ds(1, 2), halves[half]], raw.at[half, d - 1], raw_s.at[half, d - 1], raw_r.at[half, d - 1],
            across(half, d),
        )

    for e in (2, 3):
        parts[e - 1] = acc[e * TOK : (e + 1) * TOK].T.astype(BF16)
    for d in (1, 3, 2):
        for half in (0, 1):
            start(raw_copy(half, d))

    def near_copy(half):
        return remote(parts.at[0, halves[half]], near.at[half], near_s.at[half], near_r.at[half], before)

    for first, count in chunks:
        window_grads(first, count)
    parts[0] = acc[TOK : 2 * TOK].T.astype(BF16)
    start(near_copy(0))

    @pl.when(y == 0)
    def _():
        near_copy(1).start()

    x_own.wait()
    for d in range(SIDE):
        if d > 0:
            x_copy(d).wait_recv()
        xt[:, d * TOK : (d + 1) * TOK] = xa[d].T
    lat_ref[...] = acc[:TOK].T

    def mid_copy(half, d):
        return remote(
            mid.at[half, d - 1], back.at[half, d - 1], mid_s.at[half, d - 1], mid_r.at[half, d - 1],
            along(half, d),
        )

    for half in (0, 1):
        found = []
        for d in range(SIDE):
            src = ctx_at(x, y - d) if half == 0 else ctx_at(x - d, y)
            if d > 0:
                raw_copy(half, d).wait_recv()
            for e in range(2):
                part = parts[1 + e, halves[half]] if d == 0 else raw[half, d - 1, e]
                found.append((lst[2 + e, src], part.astype(F32)))
        for d in (1, 3, 2, 0):
            target = ctx_at(x + d, y) if half == 0 else ctx_at(x, y + d)
            added = None
            for entry, part in found:
                term = part * jnp.where(entry == target, 1.0, 0.0)
                added = term if added is None else added + term
            if half == 1 and d == 3:
                added += parts[0, halves[1]].astype(F32) * jnp.where(y > 0, 1.0, 0.0)
            if d == 0:
                lat_ref[halves[half]] += added
            else:
                mid[half, d - 1] = added.astype(BF16)
                start(mid_copy(half, d))

    near_copy(0).wait_recv()
    has_next = jnp.where(me < 15, 1.0, 0.0)

    @pl.when(y == SIDE - 1)
    def _():
        near_copy(1).wait_recv()
        lat_ref[LOW] += near[1].astype(F32) * has_next

    lat_ref[TOP] += near[0].astype(F32) * has_next
    for half in (0, 1):
        rows = halves[half]
        result = lat_ref[rows]
        for d in (1, 2, 3):
            mid_copy(half, d).wait_recv()
            result += back[half, d - 1].astype(F32)
        lat_ref[rows] = result
        gbuf[0, rows] = result.astype(BF16)

    spans = SPANS

    def g_copy(ch, d):
        rows = pl.ds(*spans[ch])
        return remote(gbuf.at[0, rows], gbuf.at[d, rows], g_s.at[ch, d - 1], g_r.at[ch, d - 1], along(0, d))

    def c_copy(ch):
        return remote(cs[ch], cr[ch], c_s.at[ch], c_r.at[ch], twin)

    def y_copy(ch, d):
        return remote(ys[ch].at[(y + d) % SIDE], yr[ch].at[d - 1], y_s.at[ch, d - 1], y_r.at[ch, d - 1], along(1, d))

    def z_copy(ch, d, owner):
        piece = zr[ch].at[owner]
        return remote(piece, piece, z_s.at[ch, d - 1], z_r.at[ch, d - 1], {"dp": (dp + 2 * d) % n_dp})

    def f_copy(ch, owner):
        piece = fin[ch].at[owner]
        return remote(piece, piece, f_s.at[ch], f_r.at[ch], twin)

    n_z = n_dp // 2
    part = fin[0].shape[1]

    def slot(ch, row, half):
        at, wide = divmod(ch, 2)
        return dp_v.at[at * 2 * SIDE + row * 2 + half, pl.ds(0, part), pl.ds(256 * wide, cs[ch].shape[2])]

    def multiply(ch):
        for d in (1, 2, 3):
            g_copy(ch, d).wait_recv()
        gt = jnp.concatenate([gbuf[d, pl.ds(*spans[ch])] for d in range(SIDE)], axis=1)
        weight = lax.dot_general(xt[...], gt, NT, preferred_element_type=F32)
        for i in range(2 * SIDE):
            slot(ch, i // 2, i % 2)[...] = weight[i * part : (i + 1) * part]
        for i in range(SIDE):
            cs[ch][i] = slot(ch, i, 1 - core)[...].astype(BF16)
        start(c_copy(ch))

    def add_core(ch):
        c_copy(ch).wait_recv()
        for i in range(SIDE):
            both = slot(ch, i, core)[...] + cr[ch][i].astype(F32)
            slot(ch, i, core)[...] = both
            ys[ch][i] = both.astype(BF16)
        for d in (1, 3, 2):
            start(y_copy(ch, d))

    def add_y(ch):
        added = slot(ch, y, core)[...]
        for d in (1, 2, 3):
            y_copy(ch, d).wait_recv()
            added += yr[ch][d - 1].astype(F32)
        zr[ch][z] = added.astype(BF16)
        for d in range(1, n_z):
            start(z_copy(ch, d, z))

    def add_z(ch):
        for d in range(1, n_z):
            z_copy(ch, d, (z + n_z - d) % n_z).wait_recv()
        added = zr[ch][0].astype(F32)
        for i in range(1, n_z):
            added += zr[ch][i].astype(F32)
        fin[ch][core] = added
        start(f_copy(ch, core))

    def put(ch):
        f_copy(ch, 1 - core).wait_recv()
        first, count = spans[ch]
        for i in (0, 1):
            w_ref[i * part : (i + 1) * part, first : first + count] = fin[ch][i]

    for ch in range(len(spans)):
        for d in (1, 3, 2):
            start(g_copy(ch, d))
    stages = ((0, multiply), (0, add_core), (1, add_y), (2, add_z), (3, put))
    for turn in range(len(spans) + 3):
        for late, stage_of in stages:
            if 0 <= turn - late < len(spans):
                stage_of(turn - late)
    for c in started:
        c.wait_send()

    @pl.when(y == SIDE - 1)
    def _():
        prev_copy(1).wait_send()

    @pl.when(y == 0)
    def _():
        near_copy(1).wait_send()


def deliver_kernel(lat_in, w_in, lat_out, w_out, sems):
    copies = [
        pltpu.make_async_copy(lat_in, lat_out, sems.at[0]),
        pltpu.make_async_copy(w_in, w_out, sems.at[1]),
    ]
    for c in copies:
        c.start()
    for c in copies:
        c.wait()


def deliver(lat_t, weight_grad):
    anywhere = pl.BlockSpec(memory_space=pl.ANY)
    return pl.pallas_call(
        deliver_kernel,
        out_shape=[jax.ShapeDtypeStruct(a.shape, a.dtype) for a in (lat_t, weight_grad)],
        in_specs=[anywhere, anywhere],
        out_specs=[anywhere, anywhere],
        scratch_shapes=[pltpu.SemaphoreType.DMA((2,))],
        name="deliver",
    )(lat_t, weight_grad)


def per_device(queries, latents, out_grad, layer_input, block_list):
    n_dp = lax.axis_size("dp")
    n_z = n_dp // 2
    n_heads = queries.shape[2]
    cols = layer_input.shape[2] // 16
    vmem = pl.BlockSpec(memory_space=pltpu.VMEM)
    hbm = pl.BlockSpec(memory_space=pl.ANY)
    dma = pltpu.SemaphoreType.DMA
    v = pltpu.VMEM
    widths = [count for _, count in SPANS]
    n = len(SPANS)
    part = cols // 2
    lat_t, weight_grad = pl.pallas_call(
        kernel,
        out_shape=[jax.ShapeDtypeStruct((W, TOK), F32), jax.ShapeDtypeStruct((cols, W), F32)],
        in_specs=[pl.BlockSpec(memory_space=pltpu.SMEM), hbm, hbm, hbm, hbm],
        out_specs=[vmem, vmem],
        scratch_shapes=[
            v((n_heads, W, TOK), BF16),
            v((2, TOK, HEADS, R), BF16),
            v((n_heads, TOK, R), BF16),
            v((2, SIDE, HALF, TOK), BF16),
            v((2, 3, 2, HALF, TOK), BF16),
            v((2, SIDE, 2, HALF, TOK), BF16),
            v((2, HALF, TOK), BF16),
            v((SLOTS * TOK, W), BF16),
            v((n_heads // SUB, 2 * TOK, SUB * TOK), F32),
            v((n_heads // SUB, 2 * TOK, SUB * TOK), F32),
            v((SLOTS * TOK, W), F32),
            v((3, W, TOK), BF16),
            v((2, 3, 2, HALF, TOK), BF16),
            v((2, 3, HALF, TOK), BF16),
            v((2, 3, HALF, TOK), BF16),
            v((2, HALF, TOK), BF16),
            v((SIDE, W, TOK), BF16),
            v((SIDE, TOK, SIDE * cols), BF16),
            v((SIDE * cols, SIDE * TOK), BF16),
            [v((SIDE, part, w), BF16) for w in widths],
            [v((SIDE, part, w), BF16) for w in widths],
            [v((SIDE, part, w), BF16) for w in widths],
            [v((3, part, w), BF16) for w in widths],
            [v((n_z, part, w), BF16) for w in widths],
            [v((2, part, w), F32) for w in widths],
            dma((n_heads // HEADS,)), dma((2,)), dma((2,)), dma((2, 3)), dma((2, 3)), dma((2, 3)), dma((2, 3)), dma((2,)), dma((2,)),
            dma((3,)), dma((3,)), dma, dma((2, 3)), dma((2, 3)), dma((2, 3)), dma((2, 3)), dma((2,)), dma((2,)),
            dma((n, 3)), dma((n, 3)), dma((n,)), dma((n,)), dma((n, 3)), dma((n, 3)),
            dma((n, n_z - 1)), dma((n, n_z - 1)), dma((n,)), dma((n,)),
        ],
        compiler_params=pltpu.CompilerParams(
            collective_id=0, has_side_effects=True, vmem_limit_bytes=60 * 2**20
        ),
        name="attention_backward",
    )(
        block_list[0].T,
        latents.transpose(0, 2, 1),
        queries[0].transpose(1, 2, 0),
        out_grad[0],
        layer_input[0],
    )
    lat_t, weight_grad = deliver(lat_t, weight_grad)
    return (lat_t.T[None], weight_grad)


def solution(mesh):
    placed = (
        P("dp", "ctx", None, None),
        P("dp", "ctx", None),
        P("dp", "ctx", None, None),
        P("dp", "ctx", None),
        P("dp", None, None),
    )
    return jax.shard_map(
        per_device,
        mesh=mesh,
        in_specs=placed,
        out_specs=(P("dp", "ctx", None), P("ctx", None)),
        check_vma=False,
    )
```

```python
import jax
import jax.numpy as jnp
from jax import lax
from jax.experimental import pallas as pl
from jax.experimental.pallas import tpu as pltpu
from jax.sharding import PartitionSpec as P

R = 512
W = 576
HALF = 288
TOK = 128
SLOTS = 4
SIDE = 4
HEADS = 16
SUB = 4
SPANS = ((0, 256), (256, 192), (448, 128))
SCALE = 192 ** -0.5
LOG2E = 1.4426950408889634
NT = (((1,), (1,)), ((), ()))
MESH = pl.DeviceIdType.MESH
F32 = jnp.float32
BF16 = jnp.bfloat16
TOP, LOW = pl.ds(0, HALF), pl.ds(HALF, HALF)


def place():
    me = lax.axis_index("ctx")
    return me, me // SIDE, me % SIDE


def ctx_at(x, y):
    return (x % SIDE) * SIDE + y % SIDE


def remote(src, dst, send, recv, device):
    return pltpu.make_async_remote_copy(
        src_ref=src, dst_ref=dst, send_sem=send, recv_sem=recv, device_id=device, device_id_type=MESH
    )


def greet(devices):
    barrier = pltpu.get_barrier_semaphore()
    for device in devices:
        pl.semaphore_signal(barrier, inc=1, device_id=device, device_id_type=MESH)
    pl.semaphore_wait(barrier, len(devices))


def line_peers(x, y):
    return [{"ctx": ctx_at(x + d, y)} for d in (1, 2, 3)] + [{"ctx": ctx_at(x, y + d)} for d in (1, 2, 3)]


def kernel(
    lst, lat, qt, do, inp, lat_ref, w_ref,
    q_v, stage, d_v, line, sel, got, prev, k_v, s_v, dp_v, acc, parts, raw, mid, back, near, gbuf, xa, xt,
    cs, cr, ys, yr, zr, fin,
    q_s, do_s, own_s, line_s, line_r, sel_s, sel_r, prev_s, prev_r, x_s, x_r, xo_s, raw_s, raw_r, mid_s, mid_r, near_s, near_r,
    g_s, g_r, c_s, c_r, y_s, y_r, z_s, z_r, f_s, f_r,
):
    me, x, y = place()
    dp = lax.axis_index("dp")
    n_dp = lax.axis_size("dp")
    core, z = dp % 2, dp // 2
    twin = {"dp": dp + 1 - 2 * core}
    after, before = {"ctx": (me + 1) % 16}, {"ctx": (me + 15) % 16}
    n_heads = q_v.shape[0]
    steps = n_heads // HEADS
    quarter = xa.shape[2]
    started = []

    def start(c):
        c.start()
        started.append(c)

    def do_load(i):
        return pltpu.make_async_copy(do.at[:, pl.ds(i * HEADS, HEADS)], stage.at[i % 2], do_s.at[i % 2])

    def q_load(i):
        part = pl.ds(i * HEADS, HEADS)
        return pltpu.make_async_copy(qt.at[part], q_v.at[part], q_s.at[i])

    halves = (TOP, LOW)
    chunks = ((0, 256), (256, W - 256))
    mine = (line.at[0, x], line.at[1, y])
    own_loads = [pltpu.make_async_copy(lat.at[0, halves[h]], mine[h], own_s.at[h]) for h in (0, 1)]
    for load in own_loads:
        load.start()
    do_load(0).start()
    q_load(0).start()
    x_own = pltpu.make_async_copy(
        inp.at[:, pl.ds(pl.multiple_of(x * quarter, 128), quarter)], xa.at[0], xo_s
    )
    greet(
        line_peers(x, y) + [after, before, twin] + [{"dp": (dp + 2 * d) % n_dp} for d in range(1, n_dp // 2)]
    )
    for load in own_loads:
        load.wait()

    def along(half, d):
        return {"ctx": ctx_at(x + d, y) if half == 0 else ctx_at(x, y + d)}

    def across(half, d):
        return along(1 - half, d)

    def line_copy(half, d):
        return remote(mine[half], mine[half], line_s.at[half, d - 1], line_r.at[half, d - 1], along(half, d))

    def line_wait(half, d):
        slot = line.at[0, (x + SIDE - d) % SIDE] if half == 0 else line.at[1, (y + SIDE - d) % SIDE]
        remote(slot, slot, line_s.at[half, d - 1], line_r.at[half, d - 1], along(half, d)).wait_recv()

    def prev_copy(half):
        return remote(mine[half], prev.at[half], prev_s.at[half], prev_r.at[half], after)

    for d in (1, 3, 2):
        for half in (0, 1):
            start(line_copy(half, d))
    start(prev_copy(0))

    @pl.when(y == SIDE - 1)
    def _():
        prev_copy(1).start()

    do_load(1).start()
    q_load(1).start()
    x_own.start()

    k_v[:TOK] = jnp.concatenate([line[0, x], line[1, y]], axis=0).T
    def listed(device, e):
        block = jnp.maximum(lst[2 + e, device], 0)
        return block >> 2, block & 3

    def sel_copy(half, d):
        return remote(
            sel.at[half, d - 1], got.at[half, d], sel_s.at[half, d - 1], sel_r.at[half, d - 1], across(half, d)
        )

    def pass_on():
        for half in (0, 1):
            for d in (1, 2, 3):
                line_wait(half, d)
        for d in (1, 3, 2, 0):
            for half in (0, 1):
                for e in (0, 1):
                    wanted = listed(across(half, d)["ctx"], e)[half]
                    if d == 0:
                        got[half, 0, e] = line[half, wanted]
                    else:
                        sel[half, d - 1, e] = line[half, wanted]
                if d > 0:
                    start(sel_copy(half, d))

    def columns(at):
        return (
            jnp.concatenate([q_v[at * SUB + i] for i in range(SUB)], axis=1),
            d_v[pl.ds(at * SUB, SUB)].reshape(SUB * TOK, R),
        )

    def products(keys, qc, dc):
        return (
            jnp.dot(keys, qc, preferred_element_type=F32),
            lax.dot_general(keys[:, :R], dc, NT, preferred_element_type=F32),
        )

    per = HEADS // SUB

    def arrange(i):
        do_load(i).wait()
        q_load(i).wait()
        d_v[i * HEADS : (i + 1) * HEADS] = jnp.swapaxes(stage[i % 2], 0, 1)
        if i + 2 < steps:
            do_load(i + 2).start()
            q_load(i + 2).start()

    def window_products(i, rows):
        keys = k_v[rows]
        for k in range(per):
            at = i * per + k
            s_v[at, rows], dp_v[at, rows] = products(keys, *columns(at))

    for i in range(steps // 2):
        arrange(i)
        window_products(i, pl.ds(0, TOK))
        if i == 0:
            pass_on()
    prev_copy(0).wait_recv()

    @pl.when(y == 0)
    def _():
        prev_copy(1).wait_recv()
        k_v[TOK : 2 * TOK] = jnp.concatenate([prev[0], prev[1]], axis=0).T

    @pl.when(y > 0)
    def _():
        k_v[TOK : 2 * TOK] = jnp.concatenate([prev[0], line[1, (y + SIDE - 1) % SIDE]], axis=0).T

    for i in range(steps // 2, steps):
        arrange(i)
        window_products(i, pl.ds(0, 2 * TOK))
    for i in range(steps // 2):
        window_products(i, pl.ds(TOK, TOK))
    for half in (0, 1):
        for d in (1, 2, 3):
            sel_copy(half, d).wait_recv()

    def x_copy(d):
        to = (x + d) % SIDE
        return remote(
            inp.at[:, pl.ds(pl.multiple_of(to * quarter, 128), quarter)],
            xa.at[d], x_s.at[d - 1], x_r.at[d - 1], {"ctx": ctx_at(x + d, y)},
        )

    for d in (1, 3, 2):
        start(x_copy(d))

    for e in (0, 1):
        bx, by = listed(me, e)
        k_v[(2 + e) * TOK : (3 + e) * TOK] = jnp.concatenate(
            [got[0, (y - by) & 3, e], got[1, (x - bx) & 3, e]], axis=0
        ).T
    acc[...] = jnp.zeros_like(acc)
    key_at = lax.broadcasted_iota(jnp.int32, (TOK, TOK), 0)
    tok_at = lax.broadcasted_iota(jnp.int32, (TOK, TOK), 1)
    causal = jnp.concatenate([key_at <= tok_at] * SUB, axis=1)
    away = [None] + [jnp.where(lst[e, me] >= 0, 0.0, jnp.inf) for e in range(1, SLOTS)]
    c = SCALE * LOG2E

    def softmax(at):
        qc, dc = columns(at)
        s_far, dp_far = products(k_v[2 * TOK :], qc, dc)
        ss = [s_v[at, :TOK], s_v[at, TOK:], s_far[:TOK], s_far[TOK:]]
        dprob = jnp.concatenate([dp_v[at], dp_far], axis=0)
        ss[0] = jnp.where(causal, ss[0], -jnp.inf)
        top = jnp.max(ss[0], axis=0, keepdims=True)
        for e in range(1, SLOTS):
            top = jnp.maximum(top, jnp.max(ss[e], axis=0, keepdims=True) - away[e])
        mc = top * c
        p = jnp.concatenate(
            [jnp.exp2(ss[e] * c - (mc if e == 0 else mc + away[e])) for e in range(SLOTS)], axis=0
        )
        inv = 1.0 / jnp.sum(p, axis=0, keepdims=True)
        delta = jnp.sum(p * dprob, axis=0, keepdims=True) * inv
        probs = p * inv
        dscore = probs * (dprob - delta)
        s_v[at] = probs[: 2 * TOK]
        dp_v[at] = dscore[: 2 * TOK]
        return qc, dc, probs[2 * TOK :].astype(BF16), dscore[2 * TOK :].astype(BF16)

    def grads(qc, dc, pb, ds):
        kg = lax.dot_general(ds, qc, NT, preferred_element_type=F32) * SCALE
        vg = jnp.dot(pb, dc, preferred_element_type=F32)
        acc[2 * TOK :, :R] += kg[:, :R] + vg
        acc[2 * TOK :, R:] += kg[:, R:]

    def attend(i, carry):
        held = None
        for k in range(per):
            fresh = softmax(i * per + k)
            if held is not None:
                grads(*held)
            held = fresh
        grads(*held)
        return carry

    lax.fori_loop(0, steps, attend, 0)

    def window_grads(first, count):
        values = min(count, R - first)

        def step(i, carry):
            ats = [i * per + k for k in range(per)]
            ds = jnp.concatenate([dp_v[at].astype(BF16) for at in ats], axis=1)
            pb = jnp.concatenate([s_v[at].astype(BF16) for at in ats], axis=1)
            qc = jnp.concatenate([q_v[i * HEADS + h, first : first + count] for h in range(HEADS)], axis=1)
            dc = d_v[pl.ds(i * HEADS, HEADS), :, first : first + values].reshape(HEADS * TOK, values)
            kg = lax.dot_general(ds, qc, NT, preferred_element_type=F32) * SCALE
            vg = jnp.dot(pb, dc, preferred_element_type=F32)
            acc[: 2 * TOK, first : first + values] += kg[:, :values] + vg
            if values < count:
                acc[: 2 * TOK, first + values : first + count] += kg[:, values:]
            return carry

        lax.fori_loop(0, steps, step, 0)

    def raw_copy(half, d):
        return remote(
            parts.at[pl.ds(1, 2), halves[half]], raw.at[half, d - 1], raw_s.at[half, d - 1], raw_r.at[half, d - 1],
            across(half, d),
        )

    for e in (2, 3):
        parts[e - 1] = acc[e * TOK : (e + 1) * TOK].T.astype(BF16)
    for d in (1, 3, 2):
        for half in (0, 1):
            start(raw_copy(half, d))

    def near_copy(half):
        return remote(parts.at[0, halves[half]], near.at[half], near_s.at[half], near_r.at[half], before)

    for first, count in chunks:
        window_grads(first, count)
    parts[0] = acc[TOK : 2 * TOK].T.astype(BF16)
    start(near_copy(0))

    @pl.when(y == 0)
    def _():
        near_copy(1).start()

    x_own.wait()
    for d in range(SIDE):
        if d > 0:
            x_copy(d).wait_recv()
        xt[:, d * TOK : (d + 1) * TOK] = xa[d].T
    lat_ref[...] = acc[:TOK].T

    def mid_copy(half, d):
        return remote(
            mid.at[half, d - 1], back.at[half, d - 1], mid_s.at[half, d - 1], mid_r.at[half, d - 1],
            along(half, d),
        )

    for half in (0, 1):
        found = []
        for d in range(SIDE):
            src = ctx_at(x, y - d) if half == 0 else ctx_at(x - d, y)
            if d > 0:
                raw_copy(half, d).wait_recv()
            for e in range(2):
                part = parts[1 + e, halves[half]] if d == 0 else raw[half, d - 1, e]
                found.append((lst[2 + e, src], part.astype(F32)))
        for d in (1, 3, 2, 0):
            target = ctx_at(x + d, y) if half == 0 else ctx_at(x, y + d)
            added = None
            for entry, part in found:
                term = part * jnp.where(entry == target, 1.0, 0.0)
                added = term if added is None else added + term
            if half == 1 and d == 3:
                added += parts[0, halves[1]].astype(F32) * jnp.where(y > 0, 1.0, 0.0)
            if d == 0:
                lat_ref[halves[half]] += added
            else:
                mid[half, d - 1] = added.astype(BF16)
                start(mid_copy(half, d))

    near_copy(0).wait_recv()
    has_next = jnp.where(me < 15, 1.0, 0.0)

    @pl.when(y == SIDE - 1)
    def _():
        near_copy(1).wait_recv()
        lat_ref[LOW] += near[1].astype(F32) * has_next

    lat_ref[TOP] += near[0].astype(F32) * has_next
    for half in (0, 1):
        rows = halves[half]
        result = lat_ref[rows]
        for d in (1, 2, 3):
            mid_copy(half, d).wait_recv()
            result += back[half, d - 1].astype(F32)
        lat_ref[rows] = result
        gbuf[0, rows] = result.astype(BF16)

    spans = SPANS

    def g_copy(ch, d):
        rows = pl.ds(*spans[ch])
        return remote(gbuf.at[0, rows], gbuf.at[d, rows], g_s.at[ch, d - 1], g_r.at[ch, d - 1], along(0, d))

    def c_copy(ch):
        return remote(cs[ch], cr[ch], c_s.at[ch], c_r.at[ch], twin)

    def y_copy(ch, d):
        return remote(ys[ch].at[(y + d) % SIDE], yr[ch].at[d - 1], y_s.at[ch, d - 1], y_r.at[ch, d - 1], along(1, d))

    def z_copy(ch, d, owner):
        piece = zr[ch].at[owner]
        return remote(piece, piece, z_s.at[ch, d - 1], z_r.at[ch, d - 1], {"dp": (dp + 2 * d) % n_dp})

    def f_copy(ch, owner):
        piece = fin[ch].at[owner]
        return remote(piece, piece, f_s.at[ch], f_r.at[ch], twin)

    n_z = n_dp // 2
    part = fin[0].shape[1]

    def slot(ch, row, half):
        at, wide = divmod(ch, 2)
        return dp_v.at[at * 2 * SIDE + row * 2 + half, pl.ds(0, part), pl.ds(256 * wide, cs[ch].shape[2])]

    def multiply(ch):
        for d in (1, 2, 3):
            g_copy(ch, d).wait_recv()
        gt = jnp.concatenate([gbuf[d, pl.ds(*spans[ch])] for d in range(SIDE)], axis=1)
        weight = lax.dot_general(xt[...], gt, NT, preferred_element_type=F32)
        for i in range(2 * SIDE):
            slot(ch, i // 2, i % 2)[...] = weight[i * part : (i + 1) * part]
        for i in range(SIDE):
            cs[ch][i] = slot(ch, i, 1 - core)[...].astype(BF16)
        start(c_copy(ch))

    def add_core(ch):
        c_copy(ch).wait_recv()
        for i in range(SIDE):
            both = slot(ch, i, core)[...] + cr[ch][i].astype(F32)
            slot(ch, i, core)[...] = both
            ys[ch][i] = both.astype(BF16)
        for d in (1, 3, 2):
            start(y_copy(ch, d))

    def add_y(ch):
        added = slot(ch, y, core)[...]
        for d in (1, 2, 3):
            y_copy(ch, d).wait_recv()
            added += yr[ch][d - 1].astype(F32)
        zr[ch][z] = added.astype(BF16)
        for d in range(1, n_z):
            start(z_copy(ch, d, z))

    def add_z(ch):
        for d in range(1, n_z):
            z_copy(ch, d, (z + n_z - d) % n_z).wait_recv()
        added = zr[ch][0].astype(F32)
        for i in range(1, n_z):
            added += zr[ch][i].astype(F32)
        fin[ch][core] = added
        start(f_copy(ch, core))

    def put(ch):
        f_copy(ch, 1 - core).wait_recv()
        first, count = spans[ch]
        for i in (0, 1):
            w_ref[i * part : (i + 1) * part, first : first + count] = fin[ch][i]

    for ch in range(len(spans)):
        for d in (1, 3, 2):
            start(g_copy(ch, d))
    stages = ((0, multiply), (0, add_core), (1, add_y), (2, add_z), (3, put))
    for turn in range(len(spans) + 3):
        for late, stage_of in stages:
            if 0 <= turn - late < len(spans):
                stage_of(turn - late)
    for c in started:
        c.wait_send()

    @pl.when(y == SIDE - 1)
    def _():
        prev_copy(1).wait_send()

    @pl.when(y == 0)
    def _():
        near_copy(1).wait_send()


def deliver_kernel(lat_in, w_in, lat_out, w_out):
    lat_out[...] = lat_in[...]
    w_out[...] = w_in[...]


def deliver(lat_t, weight_grad):
    vmem = pl.BlockSpec(memory_space=pltpu.VMEM)
    return pl.pallas_call(
        deliver_kernel,
        out_shape=[jax.ShapeDtypeStruct(a.shape, a.dtype) for a in (lat_t, weight_grad)],
        in_specs=[vmem, vmem],
        out_specs=[vmem, vmem],
        name="deliver",
    )(lat_t, weight_grad)


def per_device(queries, latents, out_grad, layer_input, block_list):
    n_dp = lax.axis_size("dp")
    n_z = n_dp // 2
    n_heads = queries.shape[2]
    cols = layer_input.shape[2] // 16
    vmem = pl.BlockSpec(memory_space=pltpu.VMEM)
    hbm = pl.BlockSpec(memory_space=pl.ANY)
    dma = pltpu.SemaphoreType.DMA
    v = pltpu.VMEM
    widths = [count for _, count in SPANS]
    n = len(SPANS)
    part = cols // 2
    lat_t, weight_grad = pl.pallas_call(
        kernel,
        out_shape=[jax.ShapeDtypeStruct((W, TOK), F32), jax.ShapeDtypeStruct((cols, W), F32)],
        in_specs=[pl.BlockSpec(memory_space=pltpu.SMEM), hbm, hbm, hbm, hbm],
        out_specs=[vmem, vmem],
        scratch_shapes=[
            v((n_heads, W, TOK), BF16),
            v((2, TOK, HEADS, R), BF16),
            v((n_heads, TOK, R), BF16),
            v((2, SIDE, HALF, TOK), BF16),
            v((2, 3, 2, HALF, TOK), BF16),
            v((2, SIDE, 2, HALF, TOK), BF16),
            v((2, HALF, TOK), BF16),
            v((SLOTS * TOK, W), BF16),
            v((n_heads // SUB, 2 * TOK, SUB * TOK), F32),
            v((n_heads // SUB, 2 * TOK, SUB * TOK), F32),
            v((SLOTS * TOK, W), F32),
            v((3, W, TOK), BF16),
            v((2, 3, 2, HALF, TOK), BF16),
            v((2, 3, HALF, TOK), BF16),
            v((2, 3, HALF, TOK), BF16),
            v((2, HALF, TOK), BF16),
            v((SIDE, W, TOK), BF16),
            v((SIDE, TOK, SIDE * cols), BF16),
            v((SIDE * cols, SIDE * TOK), BF16),
            [v((SIDE, part, w), BF16) for w in widths],
            [v((SIDE, part, w), BF16) for w in widths],
            [v((SIDE, part, w), BF16) for w in widths],
            [v((3, part, w), BF16) for w in widths],
            [v((n_z, part, w), BF16) for w in widths],
            [v((2, part, w), F32) for w in widths],
            dma((n_heads // HEADS,)), dma((2,)), dma((2,)), dma((2, 3)), dma((2, 3)), dma((2, 3)), dma((2, 3)), dma((2,)), dma((2,)),
            dma((3,)), dma((3,)), dma, dma((2, 3)), dma((2, 3)), dma((2, 3)), dma((2, 3)), dma((2,)), dma((2,)),
            dma((n, 3)), dma((n, 3)), dma((n,)), dma((n,)), dma((n, 3)), dma((n, 3)),
            dma((n, n_z - 1)), dma((n, n_z - 1)), dma((n,)), dma((n,)),
        ],
        compiler_params=pltpu.CompilerParams(
            collective_id=0, has_side_effects=True, vmem_limit_bytes=60 * 2**20
        ),
        name="attention_backward",
    )(
        block_list[0].T,
        latents.transpose(0, 2, 1),
        queries[0].transpose(1, 2, 0),
        out_grad[0],
        layer_input[0],
    )
    lat_t, weight_grad = deliver(lat_t, weight_grad)
    return (lat_t.T[None], weight_grad)


def solution(mesh):
    placed = (
        P("dp", "ctx", None, None),
        P("dp", "ctx", None),
        P("dp", "ctx", None, None),
        P("dp", "ctx", None),
        P("dp", None, None),
    )
    return jax.shard_map(
        per_device,
        mesh=mesh,
        in_specs=placed,
        out_specs=(P("dp", "ctx", None), P("ctx", None)),
        check_vma=False,
    )
```
